128 devices in a mesh: dp: 2 (over z_lo), expert: 64 (over y, z_hi, x, core).
Axes of the slice: x: 4, y: 4, z: 4 (z_hi: 2, z_lo: 2; z = z_hi * 2 + z_lo), core: 2. Of those that a mesh axis runs over, the one named last changes fastest.
Arguments:
- tokens: bfloat16 [16384, 2048], P(('dp', 'expert')), may hold values from -6 to 6
- out_grad: bfloat16 [16384, 2048], P(('dp', 'expert')), may hold values from -6 to 6
- expert_ids: int32 [16384, 4], P(('dp', 'expert')), may hold values from 0 to 63, all different within a row; in each aligned block of 128 rows (0 to 127, 128 to 255, ...) at most 12 rows name the same one
- gate_probs: float32 [16384, 4], P(('dp', 'expert')), may hold values from 0.05 to 0.6
- w_gate: bfloat16 [64, 2048, 768], P('expert'), may hold values from -0.125 to 0.125
- w_up: bfloat16 [64, 2048, 768], P('expert'), may hold values from -0.125 to 0.125
- w_down: bfloat16 [64, 768, 2048], P('expert'), may hold values from -0.21875 to 0.21875
Outputs:
- layer_output: bfloat16 [16384, 2048], P(('dp', 'expert'))
- input_grad: bfloat16 [16384, 2048], P(('dp', 'expert'))
- probs_grad: float32 [16384, 4], P(('dp', 'expert'))
- gate_grad: bfloat16 [64, 2048, 768], P('expert', 'dp')
- up_grad: bfloat16 [64, 2048, 768], P('expert', 'dp')
- down_grad: bfloat16 [64, 768, 2048], P('expert', None, 'dp')
The draws below stay inside these ranges and needn't reach their ends.
Inputs may be any that keep to these rules, and one draw needn't show every extreme that they name: `expert_ids`: each row names 4 different experts; within the 128 rows of one device no expert is named by more than 12 rows.
All inputs are finite; a program needn't handle non-finite values.
Results may differ from the reference program's by a relative error of at most 0.0064.
Values may be sent and summed in bfloat16 or wider, within the bound.
A program may use at most 192 MiB of HBM per device.

```python
import math
import jax
import jax.numpy as jnp
import numpy as np
from jax import lax

D = 2048
FF = 768
TOPK = 4
TOK_DEV = 128
EXPERTS = 64
CAP = 12
TOKENS = 16384
N_DP = 2
N_EXPERT = 64


def level_of(key, dims, shards, smallest, high):
    loudness = 1.0
    for axis_at, parts in shards:
        heights = jax.random.uniform(jax.random.fold_in(jax.random.fold_in(key, 6), axis_at), (parts,), jnp.float32, smallest / len(shards), high / len(shards))
        loudness = loudness * jnp.repeat(jnp.exp(heights), dims[axis_at] // parts).reshape((-1,) + (1,) * (len(dims) - 1 - axis_at))
    return loudness


def routed_block(rng, own, number, rows, number_of, top, reach, lean):
    sequence = jax.random.permutation(rng, number_of)
    heavy_load, usual = load_shares(number_of, rows * top, reach, lean, True), load_shares(number_of, rows * top, reach, lean, False)
    places = jnp.arange(number_of)

    def named(sizes, offset_by):
        used = int((sizes > 0).sum())
        fixed = max(1, used // 4)
        moved = fixed + (places - fixed + offset_by * (used - fixed)) % max(1, number_of - fixed)
        return jnp.zeros((number_of,), jnp.int32).at[sequence[jnp.where(places < fixed, places, moved)]].set(jnp.asarray(sizes, jnp.int32))

    sizes = jnp.where(number % 4 == 0, named(heavy_load, number // 4), named(usual, number - number // 4 - 1))
    mixed = jax.random.permutation(jax.random.fold_in(own, 3), number_of)
    giver, taker = mixed[0:number_of // 2 * 2:2], mixed[1:number_of // 2 * 2:2]
    room = jnp.minimum(sizes[giver] - 1, reach - sizes[taker]) // 2
    room = jnp.where((giver == sequence[0]) | (taker == sequence[0]) | (sizes[taker] == 0), 0, jnp.maximum(room, 0))
    moved = jax.random.randint(jax.random.fold_in(own, 4), (number_of // 2,), 0, 1 << 20) % (room + 1)
    sizes = sizes.at[giver].add(-moved).at[taker].add(moved)
    items = jnp.searchsorted(jnp.cumsum(sizes), jnp.arange(rows * top), side="right").astype(jnp.int32)
    listing = items.reshape(top, rows).T
    listing = listing[jax.random.permutation(jax.random.fold_in(own, 1), rows)]
    offset_by = jax.random.randint(jax.random.fold_in(own, 2), (rows, 1), 0, top)
    return jnp.take_along_axis(listing, (jnp.arange(top)[None, :] + offset_by) % top, axis=1)


def load_shares(count, total, bound, skew, full):
    loads = [(1 << 20) // math.isqrt(grade ** skew) + 1 for grade in range(1, count + 1)]
    largest = bound if full else min(bound, max(-(-total // count), total * loads[0] // sum(loads)))
    least = 1 if total - largest >= count - 1 else 0
    given, surplus = [largest] + [least] * (count - 1), total - largest - least * (count - 1)
    while surplus > 0:
        free = [i for i in range(1, count) if given[i] < largest] or [i for i in range(1, count) if given[i] < bound]
        mass, remaining = sum([loads[i] for i in free]), surplus
        for i in free:
            more = min(bound - given[i], max(1, remaining * loads[i] // mass), surplus)
            given[i] = given[i] + more
            surplus = surplus - more
    return np.array(given)


def noise(key, extent, deviation, reach, pieces=(), held_as=jnp.bfloat16):
    entries = deviation * jax.random.normal(key, extent, jnp.float32)
    if pieces:
        entries = entries * level_of(key, extent, pieces, -0.22, 0.18)
    return jnp.clip(entries, -reach, reach).astype(held_as)


def setup_inputs(seed: int = 0) -> dict:
    key_of = jax.random.split(jax.random.key(seed), 8)
    tokens = noise(key_of[0], (TOKENS, D), 1.0, 6.0, ((0, 128),))
    out_grad = noise(key_of[1], (TOKENS, D), 1.0, 6.0, ((0, 128),))
    expert_ids_keys = jax.random.split(jax.random.fold_in(key_of[2], 1), TOKENS // TOK_DEV)
    expert_ids_turns = jax.random.permutation(jax.random.fold_in(key_of[2], 3), TOKENS // TOK_DEV)
    expert_ids = jax.vmap(lambda own, number: routed_block(jax.random.fold_in(key_of[2], 2), own, number, TOK_DEV, EXPERTS, TOPK, CAP, 2))(expert_ids_keys, expert_ids_turns).reshape((TOKENS, TOPK))
    gate_probs = jnp.clip(jnp.exp(math.log(0.6) - 2.4849067 * jax.random.uniform(key_of[3], (TOKENS, TOPK), jnp.float32) ** level_of(key_of[3], (TOKENS, TOPK), ((0, 128),), -0.2, 0.2)), 0.05, 0.6)
    w_gate = noise(key_of[4], (EXPERTS, D, FF), D ** -0.5, 0.125, ((0, 64),))
    w_up = noise(key_of[5], (EXPERTS, D, FF), D ** -0.5, 0.125, ((0, 64),))
    w_down = noise(key_of[6], (EXPERTS, FF, D), FF ** -0.5, 0.21875, ((0, 64),))
    return dict(tokens=tokens, out_grad=out_grad, expert_ids=expert_ids, gate_probs=gate_probs, w_gate=w_gate, w_up=w_up, w_down=w_down)


def reference(tokens, out_grad, expert_ids, gate_probs, w_gate, w_up, w_down):
    choices = TOKENS * TOPK
    blocks = expert_ids.reshape(N_DP * N_EXPERT, TOK_DEV * TOPK)
    onehot = (blocks[:, :, None] == jnp.arange(EXPERTS, dtype=jnp.int32)[None, None, :]).astype(jnp.int32)
    ranks = jnp.sum(jnp.cumsum(onehot, 1) * onehot, 2) - 1
    block_index = jnp.arange(N_DP * N_EXPERT, dtype=jnp.int32)
    position = (block_index[:, None] * CAP + ranks).astype(jnp.int32)
    slots_each = N_DP * N_EXPERT * CAP
    flat_slot = (blocks * slots_each + position).reshape(choices).astype(jnp.int32)
    owner = jnp.full((EXPERTS * slots_each,), choices, jnp.int32)
    owner = owner.at[flat_slot].set(jnp.arange(choices, dtype=jnp.int32))
    table = owner.reshape(EXPERTS, slots_each)
    zero_row = jnp.zeros((1, D), tokens.dtype)
    token_ext = jnp.concatenate([tokens, zero_row], 0)
    scaled = (gate_probs[:, :, None] * out_grad[:, None, :].astype(jnp.float32)).astype(jnp.bfloat16)
    scaled_ext = jnp.concatenate([scaled.reshape(choices, D), zero_row.astype(jnp.bfloat16)], 0)

    def expert(operands):
        slot_owner, gate_w, up_w, down_w = operands
        rows = token_ext[slot_owner // TOPK]
        grads = scaled_ext[slot_owner]
        act_gate = jnp.dot(rows, gate_w, preferred_element_type=jnp.float32)
        act_up = jnp.dot(rows, up_w, preferred_element_type=jnp.float32)
        sig = jax.nn.sigmoid(act_gate)
        silu = act_gate * sig
        hidden = (silu * act_up).astype(jnp.bfloat16)
        out_rows = jnp.dot(hidden, down_w, preferred_element_type=jnp.float32).astype(jnp.bfloat16)
        hidden_grad = jnp.dot(grads, down_w.T, preferred_element_type=jnp.float32)
        pre_gate = (hidden_grad * act_up * sig * (1.0 + act_gate * (1.0 - sig))).astype(jnp.bfloat16)
        pre_up = (hidden_grad * silu).astype(jnp.bfloat16)
        row_grad = (jnp.dot(pre_gate, gate_w.T, preferred_element_type=jnp.float32)
                    + jnp.dot(pre_up, up_w.T, preferred_element_type=jnp.float32)).astype(jnp.bfloat16)
        grad_g = jnp.dot(rows.T, pre_gate, preferred_element_type=jnp.float32).astype(jnp.bfloat16)
        grad_u = jnp.dot(rows.T, pre_up, preferred_element_type=jnp.float32).astype(jnp.bfloat16)
        grad_d = jnp.dot(hidden.T, grads, preferred_element_type=jnp.float32).astype(jnp.bfloat16)
        return out_rows, row_grad, grad_g, grad_u, grad_d

    out_all, rowgrad_all, gate_grad, up_grad, down_grad = lax.map(expert, (table, w_gate, w_up, w_down))
    picked = out_all.reshape(EXPERTS * slots_each, D)[flat_slot].reshape(TOKENS, TOPK, D).astype(jnp.float32)
    layer_output = jnp.sum(gate_probs[:, :, None] * picked, 1).astype(jnp.bfloat16)
    probs_grad = jnp.sum(picked * out_grad[:, None, :].astype(jnp.float32), 2)
    back = rowgrad_all.reshape(EXPERTS * slots_each, D)[flat_slot].reshape(TOKENS, TOPK, D).astype(jnp.float32)
    input_grad = jnp.sum(back, 1).astype(jnp.bfloat16)
    return layer_output, input_grad, probs_grad, gate_grad, up_grad, down_grad
```

```python
import functools

import jax
import jax.numpy as jnp
import numpy as np
from jax import lax
from jax.experimental import pallas as pl
from jax.experimental.pallas import tpu as pltpu
from jax.sharding import PartitionSpec as P

MESH = pl.DeviceIdType.MESH
BF = jnp.bfloat16
F32 = jnp.float32

CAP = 12
ROWS = 16
T0, T1, G0, G1, O0, O1, R0, R1 = range(8)
SEND = {T0: 0, T1: 1, G0: 2, G1: 0, O0: 1, O1: 2, R0: 0, R1: 1}


def dot(a, b):
    return jnp.dot(a, b, preferred_element_type=F32)


def dot_nt(a, b):
    return lax.dot_general(a, b, (((1,), (1,)), ((), ())), preferred_element_type=F32)


def dot_tn(a, b):
    return lax.dot_general(a, b, (((0,), (0,)), ((), ())), preferred_element_type=F32)


def kernel(
    ids_ref, probs_ref, tok_ref, grad_ref, triu_ref, umat_ref, vmat_ref, wg_hbm, wu_hbm, wd_hbm,
    lay_out, inp_out, prb_out, gate_out, up_out, down_out, mid,
    send, recv, wg, wu, wd, rows, grads, act, hidden, pre, wide,
    ztok, zgrad, zids, zprobs, zlay_s, zinp_s, zprb_s, zlay_r, zinp_r, zprb_r,
    lay_acc, prb_acc, dprows, dppre, dpdown, dsend,
    wsem, ssem, rsem, xs, xr,
):
    tok_n, D = tok_ref.shape
    FF = wg.shape[1]
    Q = D // 4
    HALF = D // 2
    NB = recv.shape[2] * recv.shape[3] * 2
    GR = NB * CAP
    CR = GR // 2

    d = lax.axis_index("dp")
    e = lax.axis_index("expert")
    c = e % 2
    x = (e // 2) % 4
    zh = (e // 8) % 2
    y = e // 16

    def at(dp, yy, zz, xx, cc):
        return (dp, ((yy * 2 + zz) * 4 + xx) * 2 + cc)

    def px(k, dc):
        return at(d, y, zh, (x + k) % 4, (c + dc) % 2)

    def py(k, dc):
        return at(d, (y + k) % 4, zh, x, (c + dc) % 2)

    pz = at(1 - d, y, 1 - zh, x, c)
    pdp = (1 - d, e)
    pcore = at(d, y, zh, x, 1 - c)

    barrier = pltpu.get_barrier_semaphore()
    peers = [px(k, dc) for k in (1, 2, 3) for dc in (0, 1)]
    peers += [py(k, dc) for k in (1, 2, 3) for dc in (0, 1)]
    peers += [pz, pdp, pcore]
    for p in peers:
        pl.semaphore_signal(barrier, inc=1, device_id=p, device_id_type=MESH)

    weights = [
        pltpu.make_async_copy(src, dst, wsem.at[i])
        for i, (src, dst) in enumerate(((wg_hbm, wg), (wu_hbm, wu), (wd_hbm, wd)))
    ]
    for cp in weights:
        cp.start()

    pl.semaphore_wait(barrier, len(peers))

    def remote(src, dst, ss, rs, to):
        cp = pltpu.make_async_remote_copy(
            src_ref=src, dst_ref=dst, send_sem=ss, recv_sem=rs, device_id=to, device_id_type=MESH
        )
        cp.start()
        return cp

    count = [0]
    extras = []

    def extra(src, dst, to):
        i = count[0]
        count[0] += 1
        cp = remote(src, dst, xs.at[i], xr.at[i], to)
        extras.append(cp)
        return cp

    z_ids = extra(ids_ref, zids, pz)
    z_probs = extra(probs_ref, zprobs, pz)
    z_tok = extra(tok_ref, ztok, pz)
    z_grad = extra(grad_ref, zgrad, pz)

    firsts, finals = {}, {}

    def first_legs(b):
        s = SEND[b]
        mids, ends = [], []
        n = 0
        for k in (1, 3, 2):
            for dc in (0, 1):
                to = px(k, 0) if dc == 0 else py(k, 1)
                mids.append(remote(
                    send.at[s, dc, k, pl.ds(1, 3)], mid.at[b, dc, k - 1],
                    ssem.at[b, n], rsem.at[b, n], to,
                ))
                n += 1
        for k in (1, 3, 2):
            for dc in (0, 1):
                to = px(k, 0) if dc == 0 else py(k, 1)
                ends.append(remote(
                    send.at[s, dc, k, 0], recv.at[b, dc, k, 0],
                    ssem.at[b, n], rsem.at[b, n], to,
                ))
                n += 1
                to = py(k, 0) if dc == 0 else px(k, 1)
                ends.append(remote(
                    send.at[s, dc, 0, k], recv.at[b, dc, 0, k],
                    ssem.at[b, n], rsem.at[b, n], to,
                ))
                n += 1
        ends.append(remote(
            send.at[s, 1, 0, 0], recv.at[b, 1, 0, 0], ssem.at[b, n], rsem.at[b, n], pcore,
        ))
        recv[b, 0, 0, 0] = send[s, 0, 0, 0]
        firsts[b] = (mids, ends)

    def second_legs(b):
        mids, ends = firsts[b]
        for cp in mids:
            cp.wait_recv()
        n = 19
        seconds = []
        for k in (1, 3, 2):
            for dc in (0, 1):
                to = py(k, 0) if dc == 0 else px(k, 0)
                seconds.append(remote(
                    mid.at[b, dc, pl.ds(0, 3), k - 1], recv.at[b, dc, pl.ds(1, 3), k],
                    ssem.at[b, n], rsem.at[b, n], to,
                ))
                n += 1
        finals[b] = ends + seconds

    def arrived(b):
        for cp in finals[b]:
            cp.wait_recv()

    sent = set()

    def sent_first(b):
        for cp in firsts[b][0] + firsts[b][1]:
            cp.wait_send()
        sent.add(b)

    def route(ids, probs, sign):
        b = lax.broadcasted_iota(jnp.int32, (NB, tok_n), 0)
        dc = b >> 4
        k1 = (b >> 2) & 3
        k2 = b & 3
        dx = jnp.where(dc == 0, k1, k2)
        dy = jnp.where(dc == 0, k2, k1)
        ee = ((((y + sign * dy) & 3) * 2 + zh) * 4 + ((x + sign * dx) & 3)) * 2 + ((c + dc) & 1)
        named = jnp.zeros((NB, tok_n), F32)
        prob = jnp.zeros((NB, tok_n), F32)
        for k in range(4):
            hit = ids[k : k + 1, :] == ee
            named = named + jnp.where(hit, 1.0, 0.0)
            prob = prob + jnp.where(hit, probs[k : k + 1, :], 0.0)
        rank = dot(named.astype(BF), triu_ref[...])
        pos = jnp.where(named > 0.0, rank, -100.0).astype(jnp.int32)
        return ee, pos, prob

    def slots(pos):
        shape = (NB, ROWS, tok_n)
        i = lax.broadcasted_iota(jnp.int32, shape, 1)
        at_pos = jnp.broadcast_to(pos[:, None, :], shape)
        main = at_pos == i
        ext = [at_pos == (i - CAP) * 3 + s for s in range(3)]
        return main, ext

    def flat(v):
        return v.reshape(NB * ROWS, tok_n)

    def ones(mask):
        return flat(jnp.where(mask, 1.0, 0.0)).astype(BF)

    def weighted(mask, prob):
        v = flat(jnp.where(mask, jnp.broadcast_to(prob[:, None, :], mask.shape), 0.0))
        hi = v.astype(BF)
        return hi, (v - hi.astype(F32)).astype(BF)

    def seg(s):
        return pl.ds(s * Q, Q)

    def pack_tokens(b, route_of, src):
        _, pos, _ = route_of
        main, ext = slots(pos)
        main = ones(main)
        for s in range(3):
            lhs = jnp.concatenate([main, ones(ext[s])], 1)
            rhs = jnp.concatenate([src[:, seg(s)], src[:, seg(3)]], 0)
            send[SEND[b], :, :, :, :, seg(s)] = dot(lhs, rhs).astype(BF).reshape(2, 4, 4, ROWS, Q)

    def pack_grads(b, route_of, src):
        _, pos, prob = route_of
        main, ext = slots(pos)
        main_hi, main_lo = weighted(main, prob)
        for s in range(3):
            ext_hi, ext_lo = weighted(ext[s], prob)
            lhs = jnp.concatenate([main_hi, ext_hi, main_lo, ext_lo], 1)
            rhs = jnp.concatenate([src[:, seg(s)], src[:, seg(3)]], 0)
            rhs = jnp.concatenate([rhs, rhs], 0)
            send[SEND[b], :, :, :, :, seg(s)] = dot(lhs, rhs).astype(BF).reshape(2, 4, 4, ROWS, Q)

    def unpack(b, dst, w):
        for dc in range(2):
            r = pl.ds(w * GR + dc * CR, CR)
            last = jnp.zeros((CR, Q), F32)
            for s in range(3):
                piece = recv[b, dc, :, :, :, seg(s)].reshape(16 * ROWS, Q)
                dst[r, seg(s)] = dot(umat_ref[0], piece).astype(BF)
                last = last + dot(umat_ref[s + 1], piece)
            dst[r, seg(3)] = last.astype(BF)

    def pack_rows(b):
        for dc in range(2):
            r = pl.ds(dc * CR, CR)
            for s in range(3):
                piece = dot(vmat_ref[0], wide[r, seg(s)]) + dot(vmat_ref[s + 1], wide[r, seg(3)])
                send[SEND[b], dc, :, :, :, seg(s)] = piece.astype(BF).reshape(4, 4, ROWS, Q)

    TF = 256

    def forward(w, b):
        r = pl.ds(w * GR, GR)

        @pl.loop(0, FF // TF)
        def _(n):
            col = pl.ds(pl.multiple_of(n * TF, TF), TF)
            ag = dot(rows[r, :], wg[:, col])
            au = dot(rows[r, :], wu[:, col])
            act[0, r, col] = ag
            act[1, r, col] = au
            hidden[r, col] = (ag * (1.0 / (1.0 + jnp.exp(-ag))) * au).astype(BF)

        @pl.loop(0, D // Q)
        def _(n):
            col = pl.ds(pl.multiple_of(n * Q, Q), Q)
            wide[:, col] = dot(hidden[r, :], wd[:, col]).astype(BF)

        pack_rows(b)

    def backward(w, b):
        r = pl.ds(w * GR, GR)

        @pl.loop(0, FF // TF)
        def _(n):
            col = pl.ds(pl.multiple_of(n * TF, TF), TF)
            hg = dot_nt(grads[r, :], wd[col, :])
            ag = act[0, r, col]
            s = 1.0 / (1.0 + jnp.exp(-ag))
            pre[0, r, col] = (hg * act[1, r, col] * s * (1.0 + ag * (1.0 - s))).astype(BF)
            pre[1, r, col] = (hg * (ag * s)).astype(BF)

        @pl.loop(0, D // TF)
        def _(n):
            col = pl.ds(pl.multiple_of(n * TF, TF), TF)
            total = dot_nt(pre[0, r, :], wg[col, :]) + dot_nt(pre[1, r, :], wu[col, :])
            wide[:, col] = total.astype(BF)

        pack_rows(b)

    def combine_out(b, route_of, ids, g_ref, lay, prb):
        ee, pos, prob = route_of
        main, ext = slots(pos)
        main_hi, main_lo = weighted(main, prob)
        main_m = flat(jnp.where(main, 1.0, 0.0))
        last = jnp.zeros((tok_n, Q), F32)
        inner = jnp.zeros((NB * ROWS, tok_n), F32)
        for s in range(3):
            ext_hi, ext_lo = weighted(ext[s], prob)
            piece = recv[b, :, :, :, :, seg(s)].reshape(NB * ROWS, Q)
            both = dot_tn(jnp.concatenate([main_hi, ext_hi], 1), piece)
            both = both + dot_tn(jnp.concatenate([main_lo, ext_lo], 1), piece)
            lay[:, seg(s)] = both[:tok_n].astype(lay.dtype)
            last = last + both[tok_n:]
            ext_m = flat(jnp.where(ext[s], 1.0, 0.0))
            inner = inner + dot_nt(piece, g_ref[:, seg(s)]) * main_m
            inner = inner + dot_nt(piece, g_ref[:, seg(3)]) * ext_m
        lay[:, seg(3)] = last.astype(lay.dtype)
        inner = jnp.sum(inner.reshape(NB, ROWS, tok_n), 1)
        for k in range(4):
            hit = ids[k : k + 1, :] == ee
            prb[k : k + 1, :] = jnp.sum(jnp.where(hit, inner, 0.0), 0, keepdims=True)
        prb[4:8, :] = jnp.zeros((4, tok_n), F32)

    def combine_grad(b, route_of, dst):
        _, pos, _ = route_of
        main, ext = slots(pos)
        main = ones(main)
        last = jnp.zeros((tok_n, Q), F32)
        for s in range(3):
            piece = recv[b, :, :, :, :, seg(s)].reshape(NB * ROWS, Q)
            both = dot_tn(jnp.concatenate([main, ones(ext[s])], 1), piece)
            dst[:, seg(s)] = both[:tok_n].astype(dst.dtype)
            last = last + both[tok_n:]
        dst[:, seg(3)] = last.astype(dst.dtype)

    mine = pl.multiple_of(d * HALF, HALF)
    other = pl.multiple_of((1 - d) * HALF, HALF)

    def dp_rows(w):
        r = pl.ds(w * GR, GR)
        return extra(rows.at[r, pl.ds(other, HALF)], dprows.at[r], pdp)

    def dp_pre(w):
        r = pl.ds(w * GR, GR)
        return [extra(pre.at[i, r], dppre.at[i, r], pdp) for i in range(2)]

    own_ids, own_probs = ids_ref[...], probs_ref[...]
    to_own = route(own_ids, own_probs, 1)
    pack_tokens(T0, to_own, tok_ref)
    first_legs(T0)
    pack_grads(G0, to_own, grad_ref)
    z_ids.wait_recv()
    z_probs.wait_recv()
    z_ids_v, z_probs_v = zids[...], zprobs[...]
    to_z = route(z_ids_v, z_probs_v, 1)
    z_tok.wait_recv()
    pack_tokens(T1, to_z, ztok)
    first_legs(T1)
    second_legs(T0)
    first_legs(G0)
    z_grad.wait_recv()
    sent_first(T0)
    pack_grads(G1, to_z, zgrad)
    second_legs(T1)
    first_legs(G1)

    for cp in weights:
        cp.wait()
    arrived(T0)
    unpack(T0, rows, 0)
    dp_in = [dp_rows(0)]
    sent_first(T1)
    forward(0, O0)
    second_legs(G0)
    first_legs(O0)
    arrived(T1)
    unpack(T1, rows, 1)
    dp_in.append(dp_rows(1))
    sent_first(G0)
    forward(1, O1)
    second_legs(G1)
    first_legs(O1)

    arrived(G0)
    unpack(G0, grads, 0)
    sent_first(G1)
    backward(0, R0)
    dp_in += dp_pre(0)
    second_legs(O0)
    first_legs(R0)
    arrived(G1)
    unpack(G1, grads, 1)
    sent_first(O0)
    backward(1, R1)
    dp_in += dp_pre(1)
    second_legs(O1)
    first_legs(R1)

    FB = 256

    @pl.loop(0, FF // FB)
    def _(n):
        col = pl.ds(pl.multiple_of(n * FB, FB), FB)
        dsend[col, :] = dot_tn(hidden[:, col], grads[:, pl.ds(other, HALF)]).astype(BF)

    dp_down = extra(dsend, dpdown, pdp)

    arrived(O0)
    own_back = route(own_ids, own_probs, -1)
    combine_out(O0, own_back, own_ids, grad_ref, lay_acc, prb_acc)
    second_legs(R0)
    arrived(O1)
    z_back = route(z_ids_v, z_probs_v, -1)
    combine_out(O1, z_back, z_ids_v, zgrad, zlay_s, zprb_s)
    z_lay = extra(zlay_s, zlay_r, pz)
    z_prb = extra(zprb_s, zprb_r, pz)
    second_legs(R1)

    for cp in dp_in:
        cp.wait_recv()

    @pl.loop(0, HALF // FB)
    def _(n):
        at_n = pl.multiple_of(n * FB, FB)
        own = rows[:, pl.ds(mine + at_n, FB)]
        theirs = dprows[:, pl.ds(at_n, FB)]
        for i, out in enumerate((gate_out, up_out)):
            total = dot_tn(own, pre[i]) + dot_tn(theirs, dppre[i])
            out[pl.ds(at_n, FB), :] = total.astype(BF)

    arrived(R1)
    combine_grad(R1, z_back, zinp_s)
    z_inp = extra(zinp_s, zinp_r, pz)
    z_lay.wait_recv()
    lay_out[...] = (lay_acc[...] + zlay_r[...].astype(F32)).astype(BF)
    z_prb.wait_recv()
    prb_out[...] = prb_acc[...] + zprb_r[...]
    arrived(R0)
    combine_grad(R0, own_back, lay_acc)

    dp_down.wait_recv()

    @pl.loop(0, FF // FB)
    def _(n):
        col = pl.ds(pl.multiple_of(n * FB, FB), FB)
        own = dot_tn(hidden[:, col], grads[:, pl.ds(mine, HALF)])
        down_out[col, :] = (own + dpdown[col, :].astype(F32)).astype(BF)

    z_inp.wait_recv()
    inp_out[...] = (lay_acc[...] + zinp_r[...].astype(F32)).astype(BF)

    for b in range(8):
        if b not in sent:
            sent_first(b)
        for cp in finals[b][len(firsts[b][1]) :]:
            cp.wait_send()
    for cp in extras:
        cp.wait_send()


def matrices():
    u = np.zeros((4, 16, CAP, 16, ROWS), np.float32)
    v = np.zeros((4, 16, ROWS, 16, CAP), np.float32)
    for k in range(16):
        m = ((4 - k // 4) % 4) * 4 + (4 - k % 4) % 4
        for i in range(CAP):
            u[0, k, i, k, i] = 1
            v[0, m, i, k, i] = 1
            u[1 + i % 3, k, i, k, CAP + i // 3] = 1
            v[1 + i % 3, m, CAP + i // 3, k, i] = 1
    u = u.reshape(4, 16 * CAP, 16 * ROWS)
    v = v.reshape(4, 16 * ROWS, 16 * CAP)
    return jnp.asarray(u, BF), jnp.asarray(v, BF)


def per_device(tokens, out_grad, expert_ids, gate_probs, w_gate, w_up, w_down):
    tok_n, D = tokens.shape
    topk = expert_ids.shape[1]
    FF = w_gate.shape[2]
    W = 3 * D // 4
    slots = 64 * CAP
    ids = jnp.concatenate([expert_ids.T, jnp.full((8 - topk, tok_n), -1, jnp.int32)], 0)
    probs = jnp.concatenate([gate_probs.T, jnp.zeros((8 - topk, tok_n), F32)], 0)
    triu = jnp.asarray(np.triu(np.ones((tok_n, tok_n), np.float32), 1), BF)
    u, v = matrices()
    vm = pl.BlockSpec(memory_space=pltpu.VMEM)
    hbm = pl.BlockSpec(memory_space=pl.ANY)
    sds = jax.ShapeDtypeStruct
    V = pltpu.VMEM
    out = pl.pallas_call(
        kernel,
        out_shape=(
            sds((tok_n, D), BF), sds((tok_n, D), BF), sds((8, tok_n), F32),
            sds((D // 2, FF), BF), sds((D // 2, FF), BF), sds((FF, D // 2), BF),
            sds((8, 2, 3, 3, ROWS, W), BF),
        ),
        in_specs=[vm] * 7 + [hbm] * 3,
        out_specs=(vm,) * 6 + (hbm,),
        scratch_shapes=[
            V((3, 2, 4, 4, ROWS, W), BF), V((8, 2, 4, 4, ROWS, W), BF),
            V((D, FF), BF), V((D, FF), BF), V((FF, D), BF),
            V((slots, D), BF), V((slots, D), BF),
            V((2, slots, FF), F32), V((slots, FF), BF), V((2, slots, FF), BF),
            V((slots // 2, D), BF),
            V((tok_n, D), BF), V((tok_n, D), BF), V((8, tok_n), jnp.int32), V((8, tok_n), F32),
            V((tok_n, D), BF), V((tok_n, D), BF), V((8, tok_n), F32),
            V((tok_n, D), BF), V((tok_n, D), BF), V((8, tok_n), F32),
            V((tok_n, D), F32), V((8, tok_n), F32),
            V((slots, D // 2), BF), V((2, slots, FF), BF), V((FF, D // 2), BF), V((FF, D // 2), BF),
            pltpu.SemaphoreType.DMA((3,)),
            pltpu.SemaphoreType.DMA((8, 25)), pltpu.SemaphoreType.DMA((8, 25)),
            pltpu.SemaphoreType.DMA((16,)), pltpu.SemaphoreType.DMA((16,)),
        ],
        compiler_params=pltpu.CompilerParams(
            collective_id=0, has_side_effects=True, vmem_limit_bytes=63 * 2**20
        ),
        cost_estimate=pl.CostEstimate(
            flops=18 * slots * D * FF, bytes_accessed=20 * 2**20, transcendentals=2 * slots * FF
        ),
        name="moe",
    )(ids, probs, tokens, out_grad, triu, u, v, w_gate[0], w_up[0], w_down[0])
    lay, inp, prb, gate, up, down = out[:6]
    return lay, inp, prb[:topk].T, gate[None], up[None], down[None]


def solution(mesh):
    return jax.shard_map(
        per_device,
        mesh=mesh,
        in_specs=(
            P(("dp", "expert"), None),
            P(("dp", "expert"), None),
            P(("dp", "expert"), None),
            P(("dp", "expert"), None),
            P("expert", None, None),
            P("expert", None, None),
            P("expert", None, None),
        ),
        out_specs=(
            P(("dp", "expert"), None),
            P(("dp", "expert"), None),
            P(("dp", "expert"), None),
            P("expert", "dp", None),
            P("expert", "dp", None),
            P("expert", None, "dp"),
        ),
        check_vma=False,
    )
```

```python
import functools

import jax
import jax.numpy as jnp
import numpy as np
from jax import lax
from jax.experimental import pallas as pl
from jax.experimental.pallas import tpu as pltpu
from jax.sharding import PartitionSpec as P

MESH = pl.DeviceIdType.MESH
BF = jnp.bfloat16
F32 = jnp.float32

CAP = 12
ROWS = 16
T0, T1, G0, G1, O0, O1, R0, R1 = range(8)
SEND = {T0: 0, G0: 1, T1: 2, G1: 3, O0: 0, R0: 1, O1: 2, R1: 3}


def dot(a, b):
    return jnp.dot(a, b, preferred_element_type=F32)


def dot_nt(a, b):
    return lax.dot_general(a, b, (((1,), (1,)), ((), ())), preferred_element_type=F32)


def dot_tn(a, b):
    return lax.dot_general(a, b, (((0,), (0,)), ((), ())), preferred_element_type=F32)


def kernel(
    ids_ref, probs_ref, tok_ref, grad_ref, triu_ref, umat_ref, vmat_ref, wg_hbm, wu_hbm, wd_hbm,
    lay_out, inp_out, prb_out, gate_out, up_out, down_out, mid,
    send, recv, wg, wu, wd, rows, grads, act, hidden, pre, wide,
    ztok, zgrad, zids, zprobs, zlay_s, zinp_s, zprb_s, zlay_r, zinp_r, zprb_r,
    lay_acc, prb_acc, dprows, dppre, dpdown, gate_v, up_v, down_v,
    wsem, ssem, rsem, xs, xr,
):
    tok_n, D = tok_ref.shape
    FF = wg.shape[1]
    Q = D // 4
    HALF = D // 2
    NB = recv.shape[2] * recv.shape[3] * 2
    GR = NB * CAP
    CR = GR // 2

    d = lax.axis_index("dp")
    e = lax.axis_index("expert")
    c = e % 2
    x = (e // 2) % 4
    zh = (e // 8) % 2
    y = e // 16

    def at(dp, yy, zz, xx, cc):
        return (dp, ((yy * 2 + zz) * 4 + xx) * 2 + cc)

    def px(k, dc):
        return at(d, y, zh, (x + k) % 4, (c + dc) % 2)

    def py(k, dc):
        return at(d, (y + k) % 4, zh, x, (c + dc) % 2)

    pz = at(1 - d, y, 1 - zh, x, c)
    pdp = (1 - d, e)
    pcore = at(d, y, zh, x, 1 - c)

    barrier = pltpu.get_barrier_semaphore()
    peers = [px(k, dc) for k in (1, 2, 3) for dc in (0, 1)]
    peers += [py(k, dc) for k in (1, 2, 3) for dc in (0, 1)]
    peers += [pz, pdp, pcore]
    for p in peers:
        pl.semaphore_signal(barrier, inc=1, device_id=p, device_id_type=MESH)

    weights = [
        pltpu.make_async_copy(src, dst, wsem.at[i])
        for i, (src, dst) in enumerate(((wg_hbm, wg), (wu_hbm, wu), (wd_hbm, wd)))
    ]
    for cp in weights:
        cp.start()

    pl.semaphore_wait(barrier, len(peers))

    def remote(src, dst, ss, rs, to):
        cp = pltpu.make_async_remote_copy(
            src_ref=src, dst_ref=dst, send_sem=ss, recv_sem=rs, device_id=to, device_id_type=MESH
        )
        cp.start()
        return cp

    count = [0]
    extras = []

    def extra(src, dst, to):
        i = count[0]
        count[0] += 1
        cp = remote(src, dst, xs.at[i], xr.at[i], to)
        extras.append(cp)
        return cp

    z_ids = extra(ids_ref, zids, pz)
    z_probs = extra(probs_ref, zprobs, pz)
    z_tok = extra(tok_ref, ztok, pz)
    z_grad = extra(grad_ref, zgrad, pz)

    firsts, finals = {}, {}

    def first_legs(b):
        s = SEND[b]
        mids, ends = [], []
        n = 0
        for k in (1, 3, 2):
            for dc in (0, 1):
                to = px(k, 0) if dc == 0 else py(k, 1)
                mids.append(remote(
                    send.at[s, dc, k, pl.ds(1, 3)], mid.at[b, dc, k - 1],
                    ssem.at[b, n], rsem.at[b, n], to,
                ))
                n += 1
        for k in (1, 3, 2):
            for dc in (0, 1):
                to = px(k, 0) if dc == 0 else py(k, 1)
                ends.append(remote(
                    send.at[s, dc, k, 0], recv.at[b, dc, k, 0],
                    ssem.at[b, n], rsem.at[b, n], to,
                ))
                n += 1
                to = py(k, 0) if dc == 0 else px(k, 1)
                ends.append(remote(
                    send.at[s, dc, 0, k], recv.at[b, dc, 0, k],
                    ssem.at[b, n], rsem.at[b, n], to,
                ))
                n += 1
        ends.append(remote(
            send.at[s, 1, 0, 0], recv.at[b, 1, 0, 0], ssem.at[b, n], rsem.at[b, n], pcore,
        ))
        recv[b, 0, 0, 0] = send[s, 0, 0, 0]
        firsts[b] = (mids, ends)

    def second_legs(b):
        mids, ends = firsts[b]
        for cp in mids:
            cp.wait_recv()
        n = 19
        seconds = []
        for k in (1, 3, 2):
            for dc in (0, 1):
                to = py(k, 0) if dc == 0 else px(k, 0)
                seconds.append(remote(
                    mid.at[b, dc, pl.ds(0, 3), k - 1], recv.at[b, dc, pl.ds(1, 3), k],
                    ssem.at[b, n], rsem.at[b, n], to,
                ))
                n += 1
        finals[b] = ends + seconds

    def arrived(b):
        for cp in finals[b]:
            cp.wait_recv()

    sent = set()

    def sent_first(b):
        for cp in firsts[b][0] + firsts[b][1]:
            cp.wait_send()
        sent.add(b)

    def route(ids, probs, sign):
        b = lax.broadcasted_iota(jnp.int32, (NB, tok_n), 0)
        dc = b >> 4
        k1 = (b >> 2) & 3
        k2 = b & 3
        dx = jnp.where(dc == 0, k1, k2)
        dy = jnp.where(dc == 0, k2, k1)
        ee = ((((y + sign * dy) & 3) * 2 + zh) * 4 + ((x + sign * dx) & 3)) * 2 + ((c + dc) & 1)
        named = jnp.zeros((NB, tok_n), F32)
        prob = jnp.zeros((NB, tok_n), F32)
        for k in range(4):
            hit = ids[k : k + 1, :] == ee
            named = named + jnp.where(hit, 1.0, 0.0)
            prob = prob + jnp.where(hit, probs[k : k + 1, :], 0.0)
        rank = dot(named.astype(BF), triu_ref[...])
        pos = jnp.where(named > 0.0, rank, -100.0).astype(jnp.int32)
        return ee, pos, prob

    def slots(pos):
        shape = (NB, ROWS, tok_n)
        i = lax.broadcasted_iota(jnp.int32, shape, 1)
        at_pos = jnp.broadcast_to(pos[:, None, :], shape)
        main = at_pos == i
        ext = [at_pos == (i - CAP) * 3 + s for s in range(3)]
        return main, ext

    def flat(v):
        return v.reshape(NB * ROWS, tok_n)

    def ones(mask):
        return flat(jnp.where(mask, 1.0, 0.0)).astype(BF)

    def weighted(mask, prob):
        v = flat(jnp.where(mask, jnp.broadcast_to(prob[:, None, :], mask.shape), 0.0))
        hi = v.astype(BF)
        return hi, (v - hi.astype(F32)).astype(BF)

    def seg(s):
        return pl.ds(s * Q, Q)

    def pack_tokens(b, route_of, src):
        _, pos, _ = route_of
        main, ext = slots(pos)
        main = ones(main)
        for s in range(3):
            lhs = jnp.concatenate([main, ones(ext[s])], 1)
            rhs = jnp.concatenate([src[:, seg(s)], src[:, seg(3)]], 0)
            send[SEND[b], :, :, :, :, seg(s)] = dot(lhs, rhs).astype(BF).reshape(2, 4, 4, ROWS, Q)

    def pack_grads(b, route_of, src):
        _, pos, prob = route_of
        main, ext = slots(pos)
        main_hi, main_lo = weighted(main, prob)
        for s in range(3):
            ext_hi, ext_lo = weighted(ext[s], prob)
            lhs = jnp.concatenate([main_hi, ext_hi, main_lo, ext_lo], 1)
            rhs = jnp.concatenate([src[:, seg(s)], src[:, seg(3)]], 0)
            rhs = jnp.concatenate([rhs, rhs], 0)
            send[SEND[b], :, :, :, :, seg(s)] = dot(lhs, rhs).astype(BF).reshape(2, 4, 4, ROWS, Q)

    def unpack(b, dst, w):
        for dc in range(2):
            r = pl.ds(w * GR + dc * CR, CR)
            last = jnp.zeros((CR, Q), F32)
            for s in range(3):
                piece = recv[b, dc, :, :, :, seg(s)].reshape(16 * ROWS, Q)
                dst[r, seg(s)] = dot(umat_ref[0], piece).astype(BF)
                last = last + dot(umat_ref[s + 1], piece)
            dst[r, seg(3)] = last.astype(BF)

    def pack_rows(b):
        for dc in range(2):
            r = pl.ds(dc * CR, CR)
            for s in range(3):
                piece = dot(vmat_ref[0], wide[r, seg(s)]) + dot(vmat_ref[s + 1], wide[r, seg(3)])
                send[SEND[b], dc, :, :, :, seg(s)] = piece.astype(BF).reshape(4, 4, ROWS, Q)

    TF = 256

    def forward(w):
        r = pl.ds(w * GR, GR)

        @pl.loop(0, FF // TF)
        def _(n):
            col = pl.ds(pl.multiple_of(n * TF, TF), TF)
            ag = dot(rows[r, :], wg[:, col])
            au = dot(rows[r, :], wu[:, col])
            act[0, r, col] = ag
            act[1, r, col] = au
            hidden[r, col] = (ag * (1.0 / (1.0 + jnp.exp(-ag))) * au).astype(BF)

    def forward_out(w, b):
        r = pl.ds(w * GR, GR)

        @pl.loop(0, D // Q)
        def _(n):
            col = pl.ds(pl.multiple_of(n * Q, Q), Q)
            wide[:, col] = dot(hidden[r, :], wd[:, col]).astype(BF)

        pack_rows(b)

    def backward(w):
        r = pl.ds(w * GR, GR)

        @pl.loop(0, FF // TF)
        def _(n):
            col = pl.ds(pl.multiple_of(n * TF, TF), TF)
            hg = dot_nt(grads[r, :], wd[col, :])
            ag = act[0, r, col]
            s = 1.0 / (1.0 + jnp.exp(-ag))
            pre[0, r, col] = (hg * act[1, r, col] * s * (1.0 + ag * (1.0 - s))).astype(BF)
            pre[1, r, col] = (hg * (ag * s)).astype(BF)

    def backward_rows(w, b):
        r = pl.ds(w * GR, GR)

        @pl.loop(0, D // TF)
        def _(n):
            col = pl.ds(pl.multiple_of(n * TF, TF), TF)
            total = dot_nt(pre[0, r, :], wg[col, :]) + dot_nt(pre[1, r, :], wu[col, :])
            wide[:, col] = total.astype(BF)

        pack_rows(b)

    def combine_out(b, route_of, ids, g_ref, lay, prb):
        ee, pos, prob = route_of
        main, ext = slots(pos)
        main_hi, main_lo = weighted(main, prob)
        main_m = flat(jnp.where(main, 1.0, 0.0))
        last = jnp.zeros((tok_n, Q), F32)
        inner = jnp.zeros((NB * ROWS, tok_n), F32)
        for s in range(3):
            ext_hi, ext_lo = weighted(ext[s], prob)
            piece = recv[b, :, :, :, :, seg(s)].reshape(NB * ROWS, Q)
            both = dot_tn(jnp.concatenate([main_hi, ext_hi], 1), piece)
            both = both + dot_tn(jnp.concatenate([main_lo, ext_lo], 1), piece)
            lay[:, seg(s)] = both[:tok_n].astype(lay.dtype)
            last = last + both[tok_n:]
            ext_m = flat(jnp.where(ext[s], 1.0, 0.0))
            inner = inner + dot_nt(piece, g_ref[:, seg(s)]) * main_m
            inner = inner + dot_nt(piece, g_ref[:, seg(3)]) * ext_m
        lay[:, seg(3)] = last.astype(lay.dtype)
        inner = jnp.sum(inner.reshape(NB, ROWS, tok_n), 1)
        for k in range(4):
            hit = ids[k : k + 1, :] == ee
            prb[k : k + 1, :] = jnp.sum(jnp.where(hit, inner, 0.0), 0, keepdims=True)

    def combine_grad(b, route_of, dst):
        _, pos, _ = route_of
        main, ext = slots(pos)
        main = ones(main)
        last = jnp.zeros((tok_n, Q), F32)
        for s in range(3):
            piece = recv[b, :, :, :, :, seg(s)].reshape(NB * ROWS, Q)
            both = dot_tn(jnp.concatenate([main, ones(ext[s])], 1), piece)
            dst[:, seg(s)] = both[:tok_n].astype(dst.dtype)
            last = last + both[tok_n:]
        dst[:, seg(3)] = last.astype(dst.dtype)

    mine = pl.multiple_of(d * HALF, HALF)
    other = pl.multiple_of((1 - d) * HALF, HALF)

    def dp_rows(w):
        r = pl.ds(w * GR, GR)
        return extra(rows.at[r, pl.ds(other, HALF)], dprows.at[r], pdp)

    def dp_pre(w):
        r = pl.ds(w * GR, GR)
        return [extra(pre.at[i, r], dppre.at[i, r], pdp) for i in range(2)]

    FB = FF // 2

    def down_part(n, half):
        return dot_tn(hidden[:, pl.ds(n * FB, FB)], grads[:, pl.ds(half, HALF)])

    own_ids, own_probs = ids_ref[...], probs_ref[...]
    to_own = route(own_ids, own_probs, 1)
    pack_tokens(T0, to_own, tok_ref)
    first_legs(T0)
    pack_grads(G0, to_own, grad_ref)
    second_legs(T0)
    first_legs(G0)
    z_ids.wait_recv()
    z_probs.wait_recv()
    z_ids_v, z_probs_v = zids[...], zprobs[...]
    to_z = route(z_ids_v, z_probs_v, 1)
    z_tok.wait_recv()
    pack_tokens(T1, to_z, ztok)
    for cp in weights:
        cp.wait()
    arrived(T0)
    unpack(T0, rows, 0)
    dp_in = [dp_rows(0)]
    first_legs(T1)
    forward(0)
    second_legs(G0)
    sent_first(T0)
    forward_out(0, O0)
    z_grad.wait_recv()
    pack_grads(G1, to_z, zgrad)
    first_legs(G1)
    second_legs(T1)
    arrived(G0)
    unpack(G0, grads, 0)
    backward(0)
    dp_in += dp_pre(0)
    first_legs(O0)
    sent_first(G0)
    backward_rows(0, R0)
    second_legs(G1)
    arrived(T1)
    unpack(T1, rows, 1)
    dp_in.append(dp_rows(1))
    sent_first(T1)
    forward(1)
    forward_out(1, O1)
    first_legs(O1)
    second_legs(O0)
    arrived(G1)
    unpack(G1, grads, 1)
    backward(1)
    dp_in += dp_pre(1)
    sent_first(G1)
    backward_rows(1, R1)
    first_legs(R1)
    second_legs(O1)
    for n in range(2):
        wide[:, pl.ds(n * HALF, HALF)] = down_part(n, other).astype(BF)
    dp_down = extra(wide, dpdown, pdp)
    first_legs(R0)
    for n in range(2):
        own = down_part(n, mine)
        act[n, pl.ds(0, FB), :] = own[:, :FF]
        act[n, pl.ds(FB, FB), pl.ds(0, HALF - FF)] = own[:, FF:]
    second_legs(R1)
    own_back = route(own_ids, own_probs, -1)
    z_back = route(z_ids_v, z_probs_v, -1)
    arrived(O1)
    combine_out(O1, z_back, z_ids_v, zgrad, zlay_s, zprb_s)
    z_lay = extra(zlay_s, zlay_r, pz)
    z_prb = extra(zprb_s, zprb_r, pz)
    arrived(O0)
    combine_out(O0, own_back, own_ids, grad_ref, lay_acc, prb_acc)
    second_legs(R0)
    arrived(R1)
    combine_grad(R1, z_back, zinp_s)
    z_inp = extra(zinp_s, zinp_r, pz)
    z_lay.wait_recv()
    lay_out[...] = (lay_acc[...] + zlay_r[...].astype(F32)).astype(BF)
    z_prb.wait_recv()
    prb_out[...] = prb_acc[...] + zprb_r[...]

    for cp in dp_in:
        cp.wait_recv()

    TG = 256

    @pl.loop(0, HALF // TG)
    def _(n):
        at_n = pl.multiple_of(n * TG, TG)
        own = rows[:, pl.ds(mine + at_n, TG)]
        theirs = dprows[:, pl.ds(at_n, TG)]
        for i, out in enumerate((gate_v, up_v)):
            total = dot_tn(own, pre[i]) + dot_tn(theirs, dppre[i])
            out[pl.ds(at_n, TG), :] = total.astype(BF)

    stores = [pltpu.make_async_copy(gate_v, gate_out, wsem.at[0])]
    stores.append(pltpu.make_async_copy(up_v, up_out, wsem.at[1]))
    for cp in stores:
        cp.start()

    arrived(R0)
    combine_grad(R0, own_back, lay_acc)
    z_inp.wait_recv()
    inp_out[...] = (lay_acc[...] + zinp_r[...].astype(F32)).astype(BF)

    dp_down.wait_recv()
    for n in range(2):
        theirs = dpdown[:, pl.ds(n * HALF, HALF)].astype(F32)
        r = pl.ds(n * FB, FB)
        down_v[r, pl.ds(0, FF)] = (act[n, pl.ds(0, FB), :] + theirs[:, :FF]).astype(BF)
        own = act[n, pl.ds(FB, FB), pl.ds(0, HALF - FF)]
        down_v[r, pl.ds(FF, HALF - FF)] = (own + theirs[:, FF:]).astype(BF)
    cp = pltpu.make_async_copy(down_v, down_out, wsem.at[2])
    cp.start()
    stores.append(cp)

    for b in range(8):
        if b not in sent:
            sent_first(b)
        for cp in finals[b][len(firsts[b][1]) :]:
            cp.wait_send()
    for cp in extras:
        cp.wait_send()
    for cp in stores:
        cp.wait()


PARTS = 2


def hand_over(*refs):
    srcs, dsts, held, sem = refs[:6], refs[6:12], refs[12:18], refs[18]
    loads, stores = [], []
    for i in range(6):
        parts = PARTS if srcs[i].shape[0] % (16 * PARTS) == 0 else 1
        n = srcs[i].shape[0] // parts
        for j in range(parts):
            r = pl.ds(j * n, n)
            loads.append(pltpu.make_async_copy(srcs[i].at[r], held[i].at[r], sem.at[0, i, j]))
            stores.append(pltpu.make_async_copy(held[i].at[r], dsts[i].at[r], sem.at[1, i, j]))
    for cp in loads:
        cp.start()
    for load, store in zip(loads, stores):
        load.wait()
        store.start()
    for cp in stores:
        cp.wait()


def matrices():
    u = np.zeros((4, 16, CAP, 16, ROWS), np.float32)
    v = np.zeros((4, 16, ROWS, 16, CAP), np.float32)
    for k in range(16):
        m = ((4 - k // 4) % 4) * 4 + (4 - k % 4) % 4
        for i in range(CAP):
            u[0, k, i, k, i] = 1
            v[0, m, i, k, i] = 1
            u[1 + i % 3, k, i, k, CAP + i // 3] = 1
            v[1 + i % 3, m, CAP + i // 3, k, i] = 1
    u = u.reshape(4, 16 * CAP, 16 * ROWS)
    v = v.reshape(4, 16 * ROWS, 16 * CAP)
    return jnp.asarray(u, BF), jnp.asarray(v, BF)


def per_device(tokens, out_grad, expert_ids, gate_probs, w_gate, w_up, w_down):
    tok_n, D = tokens.shape
    topk = expert_ids.shape[1]
    FF = w_gate.shape[2]
    W = 3 * D // 4
    slots = 64 * CAP
    ids, probs = expert_ids.T, gate_probs.T
    triu = jnp.asarray(np.triu(np.ones((tok_n, tok_n), np.float32), 1), BF)
    u, v = matrices()
    vm = pl.BlockSpec(memory_space=pltpu.VMEM)
    hbm = pl.BlockSpec(memory_space=pl.ANY)
    sds = jax.ShapeDtypeStruct
    V = pltpu.VMEM
    out = pl.pallas_call(
        kernel,
        out_shape=(
            sds((tok_n, D), BF), sds((tok_n, D), BF), sds((topk, tok_n), F32),
            sds((D // 2, FF), BF), sds((D // 2, FF), BF), sds((FF, D // 2), BF),
            sds((8, 2, 3, 3, ROWS, W), BF),
        ),
        in_specs=[vm] * 7 + [hbm] * 3,
        out_specs=(vm,) * 3 + (hbm,) * 4,
        scratch_shapes=[
            V((4, 2, 4, 4, ROWS, W), BF), V((8, 2, 4, 4, ROWS, W), BF),
            V((D, FF), BF), V((D, FF), BF), V((FF, D), BF),
            V((slots, D), BF), V((slots, D), BF),
            V((2, slots, FF), F32), V((slots, FF), BF), V((2, slots, FF), BF),
            V((slots // 2, D), BF),
            V((tok_n, D), BF), V((tok_n, D), BF), V((topk, tok_n), jnp.int32), V((topk, tok_n), F32),
            V((tok_n, D), BF), V((tok_n, D), BF), V((topk, tok_n), F32),
            V((tok_n, D), BF), V((tok_n, D), BF), V((topk, tok_n), F32),
            V((tok_n, D), F32), V((topk, tok_n), F32),
            V((slots, D // 2), BF), V((2, slots, FF), BF), V((slots // 2, D), BF),
            V((D // 2, FF), BF), V((D // 2, FF), BF), V((FF, D // 2), BF),
            pltpu.SemaphoreType.DMA((3,)),
            pltpu.SemaphoreType.DMA((8, 25)), pltpu.SemaphoreType.DMA((8, 25)),
            pltpu.SemaphoreType.DMA((16,)), pltpu.SemaphoreType.DMA((16,)),
        ],
        compiler_params=pltpu.CompilerParams(
            collective_id=0, has_side_effects=True, vmem_limit_bytes=63 * 2**20
        ),
        cost_estimate=pl.CostEstimate(
            flops=18 * slots * D * FF, bytes_accessed=20 * 2**20, transcendentals=2 * slots * FF
        ),
        name="moe",
    )(ids, probs, tokens, out_grad, triu, u, v, w_gate[0], w_up[0], w_down[0])
    lay, inp, prb, gate, up, down = pl.pallas_call(
        hand_over,
        out_shape=[sds(o.shape, o.dtype) for o in out[:6]],
        in_specs=[hbm] * 6,
        out_specs=[hbm] * 6,
        scratch_shapes=[V(o.shape, o.dtype) for o in out[:6]] + [pltpu.SemaphoreType.DMA((2, 6, PARTS))],
        name="hand_over",
    )(*out[:6])
    return lay, inp, prb.T, gate[None], up[None], down[None]


def solution(mesh):
    return jax.shard_map(
        per_device,
        mesh=mesh,
        in_specs=(
            P(("dp", "expert"), None),
            P(("dp", "expert"), None),
            P(("dp", "expert"), None),
            P(("dp", "expert"), None),
            P("expert", None, None),
            P("expert", None, None),
            P("expert", None, None),
        ),
        out_specs=(
            P(("dp", "expert"), None),
            P(("dp", "expert"), None),
            P(("dp", "expert"), None),
            P("expert", "dp", None),
            P("expert", "dp", None),
            P("expert", None, "dp"),
        ),
        check_vma=False,
    )
```

```python
import functools

import jax
import jax.numpy as jnp
import numpy as np
from jax import lax
from jax.experimental import pallas as pl
from jax.experimental.pallas import tpu as pltpu
from jax.sharding import PartitionSpec as P

MESH = pl.DeviceIdType.MESH
BF = jnp.bfloat16
F32 = jnp.float32

CAP = 12
ROWS = 16
T0, T1, G0, G1, O0, O1, R0, R1 = range(8)
SEND = {T0: 0, T1: 1, G0: 2, G1: 3, O0: 0, O1: 1, R0: 2, R1: 3}


def dot(a, b):
    return jnp.dot(a, b, preferred_element_type=F32)


def dot_nt(a, b):
    return lax.dot_general(a, b, (((1,), (1,)), ((), ())), preferred_element_type=F32)


def dot_tn(a, b):
    return lax.dot_general(a, b, (((0,), (0,)), ((), ())), preferred_element_type=F32)


def kernel(
    ids_ref, probs_ref, tok_ref, grad_ref, triu_ref, umat_ref, vmat_ref, wg_hbm, wu_hbm, wd_hbm,
    lay_out, inp_out, prb_out, gate_out, up_out, down_out, mid,
    send, recv, wg, wu, wd, rows, grads, act, hidden, pre, wide,
    ztok, zgrad, zids, zprobs, zlay_s, zinp_s, zprb_s, zlay_r, zinp_r, zprb_r,
    lay_acc, prb_acc, dprows, dppre, dpdown,
    wsem, ssem, rsem, xs, xr,
):
    tok_n, D = tok_ref.shape
    FF = wg.shape[1]
    Q = D // 4
    HALF = D // 2
    NB = recv.shape[2] * recv.shape[3] * 2
    GR = NB * CAP
    CR = GR // 2

    d = lax.axis_index("dp")
    e = lax.axis_index("expert")
    c = e % 2
    x = (e // 2) % 4
    zh = (e // 8) % 2
    y = e // 16

    def at(dp, yy, zz, xx, cc):
        return (dp, ((yy * 2 + zz) * 4 + xx) * 2 + cc)

    def px(k, dc):
        return at(d, y, zh, (x + k) % 4, (c + dc) % 2)

    def py(k, dc):
        return at(d, (y + k) % 4, zh, x, (c + dc) % 2)

    pz = at(1 - d, y, 1 - zh, x, c)
    pdp = (1 - d, e)
    pcore = at(d, y, zh, x, 1 - c)

    barrier = pltpu.get_barrier_semaphore()
    peers = [px(k, dc) for k in (1, 2, 3) for dc in (0, 1)]
    peers += [py(k, dc) for k in (1, 2, 3) for dc in (0, 1)]
    peers += [pz, pdp, pcore]
    for p in peers:
        pl.semaphore_signal(barrier, inc=1, device_id=p, device_id_type=MESH)

    weights = [
        pltpu.make_async_copy(src, dst, wsem.at[i])
        for i, (src, dst) in enumerate(((wg_hbm, wg), (wu_hbm, wu), (wd_hbm, wd)))
    ]
    for cp in weights:
        cp.start()

    def remote(src, dst, ss, rs, to):
        cp = pltpu.make_async_remote_copy(
            src_ref=src, dst_ref=dst, send_sem=ss, recv_sem=rs, device_id=to, device_id_type=MESH
        )
        cp.start()
        return cp

    count = [0]
    extras = []

    def extra(src, dst, to):
        i = count[0]
        count[0] += 1
        cp = remote(src, dst, xs.at[i], xr.at[i], to)
        extras.append(cp)
        return cp

    firsts, finals = {}, {}

    def first_legs(b):
        s = SEND[b]
        mids, ends = [], []
        n = 0
        for k in (1, 3, 2):
            for dc in (0, 1):
                to = px(k, 0) if dc == 0 else py(k, 1)
                mids.append(remote(
                    send.at[s, dc, k, pl.ds(1, 3)], mid.at[b, dc, k - 1],
                    ssem.at[b, n], rsem.at[b, n], to,
                ))
                n += 1
        for k in (1, 3, 2):
            for dc in (0, 1):
                to = px(k, 0) if dc == 0 else py(k, 1)
                ends.append(remote(
                    send.at[s, dc, k, 0], recv.at[b, dc, k, 0],
                    ssem.at[b, n], rsem.at[b, n], to,
                ))
                n += 1
                to = py(k, 0) if dc == 0 else px(k, 1)
                ends.append(remote(
                    send.at[s, dc, 0, k], recv.at[b, dc, 0, k],
                    ssem.at[b, n], rsem.at[b, n], to,
                ))
                n += 1
        ends.append(remote(
            send.at[s, 1, 0, 0], recv.at[b, 1, 0, 0], ssem.at[b, n], rsem.at[b, n], pcore,
        ))
        recv[b, 0, 0, 0] = send[s, 0, 0, 0]
        firsts[b] = (mids, ends)

    def second_legs(b):
        mids, ends = firsts[b]
        for cp in mids:
            cp.wait_recv()
        n = 19
        seconds = []
        for k in (1, 3, 2):
            for dc in (0, 1):
                to = py(k, 0) if dc == 0 else px(k, 0)
                seconds.append(remote(
                    mid.at[b, dc, pl.ds(0, 3), k - 1], recv.at[b, dc, pl.ds(1, 3), k],
                    ssem.at[b, n], rsem.at[b, n], to,
                ))
                n += 1
        finals[b] = ends + seconds

    def arrived(b):
        for cp in finals[b]:
            cp.wait_recv()

    sent = set()

    def sent_first(b):
        for cp in firsts[b][0] + firsts[b][1]:
            cp.wait_send()
        sent.add(b)

    def route(ids, probs, sign):
        b = lax.broadcasted_iota(jnp.int32, (NB, tok_n), 0)
        dc = b >> 4
        k1 = (b >> 2) & 3
        k2 = b & 3
        dx = jnp.where(dc == 0, k1, k2)
        dy = jnp.where(dc == 0, k2, k1)
        ee = ((((y + sign * dy) & 3) * 2 + zh) * 4 + ((x + sign * dx) & 3)) * 2 + ((c + dc) & 1)
        named = jnp.zeros((NB, tok_n), F32)
        prob = jnp.zeros((NB, tok_n), F32)
        for k in range(4):
            hit = ids[k : k + 1, :] == ee
            named = named + jnp.where(hit, 1.0, 0.0)
            prob = prob + jnp.where(hit, probs[k : k + 1, :], 0.0)
        rank = dot(named.astype(BF), triu_ref[...])
        pos = jnp.where(named > 0.0, rank, -100.0).astype(jnp.int32)
        return ee, pos, prob

    def slots(pos):
        shape = (NB, ROWS, tok_n)
        i = lax.broadcasted_iota(jnp.int32, shape, 1)
        at_pos = jnp.broadcast_to(pos[:, None, :], shape)
        main = at_pos == i
        ext = [at_pos == (i - CAP) * 3 + s for s in range(3)]
        return main, ext

    def flat(v):
        return v.reshape(NB * ROWS, tok_n)

    def ones(mask):
        return flat(jnp.where(mask, 1.0, 0.0)).astype(BF)

    def weighted(mask, prob):
        v = flat(jnp.where(mask, jnp.broadcast_to(prob[:, None, :], mask.shape), 0.0))
        hi = v.astype(BF)
        return hi, (v - hi.astype(F32)).astype(BF)

    def seg(s):
        return pl.ds(s * Q, Q)

    def pack_tokens(b, route_of, src):
        _, pos, _ = route_of
        main, ext = slots(pos)
        main = ones(main)
        for s in range(3):
            lhs = jnp.concatenate([main, ones(ext[s])], 1)
            rhs = jnp.concatenate([src[:, seg(s)], src[:, seg(3)]], 0)
            send[SEND[b], :, :, :, :, seg(s)] = dot(lhs, rhs).astype(BF).reshape(2, 4, 4, ROWS, Q)

    def pack_grads(b, route_of, src):
        _, pos, prob = route_of
        main, ext = slots(pos)
        main_hi, main_lo = weighted(main, prob)
        for s in range(3):
            ext_hi, ext_lo = weighted(ext[s], prob)
            lhs = jnp.concatenate([main_hi, ext_hi, main_lo, ext_lo], 1)
            rhs = jnp.concatenate([src[:, seg(s)], src[:, seg(3)]], 0)
            rhs = jnp.concatenate([rhs, rhs], 0)
            send[SEND[b], :, :, :, :, seg(s)] = dot(lhs, rhs).astype(BF).reshape(2, 4, 4, ROWS, Q)

    def unpack(b, dst, w):
        for dc in range(2):
            r = pl.ds(w * GR + dc * CR, CR)
            last = jnp.zeros((CR, Q), F32)
            for s in range(3):
                piece = recv[b, dc, :, :, :, seg(s)].reshape(16 * ROWS, Q)
                dst[r, seg(s)] = dot(umat_ref[0], piece).astype(BF)
                last = last + dot(umat_ref[s + 1], piece)
            dst[r, seg(3)] = last.astype(BF)

    def pack_rows(b):
        for dc in range(2):
            r = pl.ds(dc * CR, CR)
            for s in range(3):
                piece = dot(vmat_ref[0], wide[r, seg(s)]) + dot(vmat_ref[s + 1], wide[r, seg(3)])
                send[SEND[b], dc, :, :, :, seg(s)] = piece.astype(BF).reshape(4, 4, ROWS, Q)

    TF = 256

    def forward(w):
        r = pl.ds(w * GR, GR)

        @pl.loop(0, FF // TF)
        def _(n):
            col = pl.ds(pl.multiple_of(n * TF, TF), TF)
            ag = dot(rows[r, :], wg[:, col])
            au = dot(rows[r, :], wu[:, col])
            act[0, r, col] = ag
            act[1, r, col] = au
            hidden[r, col] = (ag * (1.0 / (1.0 + jnp.exp(-ag))) * au).astype(BF)

    def forward_out(w, b):
        r = pl.ds(w * GR, GR)

        @pl.loop(0, D // Q)
        def _(n):
            col = pl.ds(pl.multiple_of(n * Q, Q), Q)
            wide[:, col] = dot(hidden[r, :], wd[:, col]).astype(BF)

        pack_rows(b)

    def backward(w):
        r = pl.ds(w * GR, GR)

        @pl.loop(0, FF // TF)
        def _(n):
            col = pl.ds(pl.multiple_of(n * TF, TF), TF)
            hg = dot_nt(grads[r, :], wd[col, :])
            ag = act[0, r, col]
            s = 1.0 / (1.0 + jnp.exp(-ag))
            pre[0, r, col] = (hg * act[1, r, col] * s * (1.0 + ag * (1.0 - s))).astype(BF)
            pre[1, r, col] = (hg * (ag * s)).astype(BF)

    def backward_rows(w, b):
        r = pl.ds(w * GR, GR)

        @pl.loop(0, D // TF)
        def _(n):
            col = pl.ds(pl.multiple_of(n * TF, TF), TF)
            total = dot_nt(pre[0, r, :], wg[col, :]) + dot_nt(pre[1, r, :], wu[col, :])
            wide[:, col] = total.astype(BF)

        pack_rows(b)

    def combine_out(b, route_of, ids, g_ref, lay, prb):
        ee, pos, prob = route_of
        main, ext = slots(pos)
        main_hi, main_lo = weighted(main, prob)
        main_m = flat(jnp.where(main, 1.0, 0.0))
        last = jnp.zeros((tok_n, Q), F32)
        inner = jnp.zeros((NB * ROWS, tok_n), F32)
        for s in range(3):
            ext_hi, ext_lo = weighted(ext[s], prob)
            piece = recv[b, :, :, :, :, seg(s)].reshape(NB * ROWS, Q)
            both = dot_tn(jnp.concatenate([main_hi, ext_hi], 1), piece)
            both = both + dot_tn(jnp.concatenate([main_lo, ext_lo], 1), piece)
            lay[:, seg(s)] = both[:tok_n].astype(lay.dtype)
            last = last + both[tok_n:]
            ext_m = flat(jnp.where(ext[s], 1.0, 0.0))
            inner = inner + dot_nt(piece, g_ref[:, seg(s)]) * main_m
            inner = inner + dot_nt(piece, g_ref[:, seg(3)]) * ext_m
        lay[:, seg(3)] = last.astype(lay.dtype)
        inner = jnp.sum(inner.reshape(NB, ROWS, tok_n), 1)
        for k in range(4):
            hit = ids[k : k + 1, :] == ee
            prb[k : k + 1, :] = jnp.sum(jnp.where(hit, inner, 0.0), 0, keepdims=True)

    def sum_matrices(route_of):
        main, ext = slots(route_of[1])
        main = ones(main)
        return [jnp.concatenate([main, ones(ext[s])], 1) for s in range(3)]

    def combine_grad(b, sums, dst):
        last = jnp.zeros((tok_n, Q), F32)
        for s in range(3):
            piece = recv[b, :, :, :, :, seg(s)].reshape(NB * ROWS, Q)
            both = dot_tn(sums[s], piece)
            dst[:, seg(s)] = both[:tok_n].astype(dst.dtype)
            last = last + both[tok_n:]
        dst[:, seg(3)] = last.astype(dst.dtype)

    mine = pl.multiple_of(d * HALF, HALF)
    other = pl.multiple_of((1 - d) * HALF, HALF)

    def dp_rows(w):
        r = pl.ds(w * GR, GR)
        return extra(rows.at[r, pl.ds(other, HALF)], dprows.at[r], pdp)

    def dp_pre(w):
        r = pl.ds(w * GR, GR)
        return [extra(pre.at[i, r], dppre.at[i, r], pdp) for i in range(2)]

    FB = FF // 2

    def down_part(n, half):
        return dot_tn(hidden[:, pl.ds(n * FB, FB)], grads[:, pl.ds(half, HALF)])

    own_ids, own_probs = ids_ref[...], probs_ref[...]
    to_own = route(own_ids, own_probs, 1)
    pack_tokens(T0, to_own, tok_ref)
    pl.semaphore_wait(barrier, len(peers))
    z_ids = extra(ids_ref, zids, pz)
    z_probs = extra(probs_ref, zprobs, pz)
    z_tok = extra(tok_ref, ztok, pz)
    z_grad = extra(grad_ref, zgrad, pz)
    first_legs(T0)
    pack_grads(G0, to_own, grad_ref)
    z_ids.wait_recv()
    z_probs.wait_recv()
    z_ids_v, z_probs_v = zids[...], zprobs[...]
    to_z = route(z_ids_v, z_probs_v, 1)
    second_legs(T0)
    z_tok.wait_recv()
    pack_tokens(T1, to_z, ztok)
    first_legs(T1)
    for cp in weights:
        cp.wait()
    arrived(T0)
    unpack(T0, rows, 0)
    dp_in = [dp_rows(0)]
    first_legs(G0)
    second_legs(T1)
    forward(0)
    sent_first(T0)
    forward_out(0, O0)
    z_grad.wait_recv()
    pack_grads(G1, to_z, zgrad)
    second_legs(G0)
    first_legs(G1)
    arrived(T1)
    unpack(T1, rows, 1)
    dp_in.append(dp_rows(1))
    forward(1)
    sent_first(T1)
    forward_out(1, O1)
    second_legs(G1)
    first_legs(O0)
    arrived(G0)
    unpack(G0, grads, 0)
    backward(0)
    dp_in += dp_pre(0)
    sent_first(G0)
    backward_rows(0, R0)
    first_legs(O1)
    second_legs(O0)
    arrived(G1)
    unpack(G1, grads, 1)
    backward(1)
    dp_in += dp_pre(1)
    sent_first(G1)
    backward_rows(1, R1)
    first_legs(R1)
    second_legs(O1)
    for n in range(2):
        wide[:, pl.ds(n * HALF, HALF)] = down_part(n, other).astype(BF)
    dp_down = extra(wide, dpdown, pdp)
    first_legs(R0)
    for n in range(2):
        own = down_part(n, mine)
        act[n, pl.ds(0, FB), :] = own[:, :FF]
        act[n, pl.ds(FB, FB), pl.ds(0, HALF - FF)] = own[:, FF:]
    second_legs(R1)
    own_back = route(own_ids, own_probs, -1)
    z_back = route(z_ids_v, z_probs_v, -1)
    arrived(O1)
    combine_out(O1, z_back, z_ids_v, zgrad, zlay_s, zprb_s)
    z_lay = extra(zlay_s, zlay_r, pz)
    z_prb = extra(zprb_s, zprb_r, pz)
    arrived(O0)
    combine_out(O0, own_back, own_ids, grad_ref, lay_acc, prb_acc)
    second_legs(R0)
    z_sums = sum_matrices(z_back)
    arrived(R1)
    combine_grad(R1, z_sums, zinp_s)
    z_inp = extra(zinp_s, zinp_r, pz)
    z_lay.wait_recv()
    lay_out[...] = (lay_acc[...] + zlay_r[...].astype(F32)).astype(BF)
    z_prb.wait_recv()
    prb_out[...] = prb_acc[...] + zprb_r[...]

    for cp in dp_in:
        cp.wait_recv()

    TG = 256

    @pl.loop(0, HALF // TG)
    def _(n):
        at_n = pl.multiple_of(n * TG, TG)
        own = rows[:, pl.ds(mine + at_n, TG)]
        theirs = dprows[:, pl.ds(at_n, TG)]
        for i, out in enumerate((gate_out, up_out)):
            total = dot_tn(own, pre[i]) + dot_tn(theirs, dppre[i])
            out[pl.ds(at_n, TG), :] = total.astype(BF)

    own_sums = sum_matrices(own_back)
    arrived(R0)
    combine_grad(R0, own_sums, lay_acc)
    z_inp.wait_recv()
    inp_out[...] = (lay_acc[...] + zinp_r[...].astype(F32)).astype(BF)

    dp_down.wait_recv()
    for n in range(2):
        theirs = dpdown[:, pl.ds(n * HALF, HALF)].astype(F32)
        r = pl.ds(n * FB, FB)
        down_out[r, pl.ds(0, FF)] = (act[n, pl.ds(0, FB), :] + theirs[:, :FF]).astype(BF)
        own = act[n, pl.ds(FB, FB), pl.ds(0, HALF - FF)]
        down_out[r, pl.ds(FF, HALF - FF)] = (own + theirs[:, FF:]).astype(BF)
    for b in range(8):
        if b not in sent:
            sent_first(b)
        for cp in finals[b][len(firsts[b][1]) :]:
            cp.wait_send()
    for cp in extras:
        cp.wait_send()


def hand_over(*refs):
    sem = refs[12]
    copies = [pltpu.make_async_copy(refs[i], refs[6 + i], sem.at[i]) for i in range(6)]
    for cp in copies:
        cp.start()
    for cp in copies:
        cp.wait()


def matrices():
    u = np.zeros((4, 16, CAP, 16, ROWS), np.float32)
    v = np.zeros((4, 16, ROWS, 16, CAP), np.float32)
    for k in range(16):
        m = ((4 - k // 4) % 4) * 4 + (4 - k % 4) % 4
        for i in range(CAP):
            u[0, k, i, k, i] = 1
            v[0, m, i, k, i] = 1
            u[1 + i % 3, k, i, k, CAP + i // 3] = 1
            v[1 + i % 3, m, CAP + i // 3, k, i] = 1
    u = u.reshape(4, 16 * CAP, 16 * ROWS)
    v = v.reshape(4, 16 * ROWS, 16 * CAP)
    return jnp.asarray(u, BF), jnp.asarray(v, BF)


def per_device(tokens, out_grad, expert_ids, gate_probs, w_gate, w_up, w_down):
    tok_n, D = tokens.shape
    topk = expert_ids.shape[1]
    FF = w_gate.shape[2]
    W = 3 * D // 4
    slots = 64 * CAP
    ids, probs = expert_ids.T, gate_probs.T
    triu = jnp.asarray(np.triu(np.ones((tok_n, tok_n), np.float32), 1), BF)
    u, v = matrices()
    vm = pl.BlockSpec(memory_space=pltpu.VMEM)
    hbm = pl.BlockSpec(memory_space=pl.ANY)
    sds = jax.ShapeDtypeStruct
    V = pltpu.VMEM
    out = pl.pallas_call(
        kernel,
        out_shape=(
            V((tok_n, D), BF), V((tok_n, D), BF), V((topk, tok_n), F32),
            V((D // 2, FF), BF), V((D // 2, FF), BF), V((FF, D // 2), BF),
            sds((8, 2, 3, 3, ROWS, W), BF),
        ),
        in_specs=[vm] * 7 + [hbm] * 3,
        out_specs=(vm,) * 6 + (hbm,),
        scratch_shapes=[
            V((4, 2, 4, 4, ROWS, W), BF), V((8, 2, 4, 4, ROWS, W), BF),
            V((D, FF), BF), V((D, FF), BF), V((FF, D), BF),
            V((slots, D), BF), V((slots, D), BF),
            V((2, slots, FF), F32), V((slots, FF), BF), V((2, slots, FF), BF),
            V((slots // 2, D), BF),
            V((tok_n, D), BF), V((tok_n, D), BF), V((topk, tok_n), jnp.int32), V((topk, tok_n), F32),
            V((tok_n, D), BF), V((tok_n, D), BF), V((topk, tok_n), F32),
            V((tok_n, D), BF), V((tok_n, D), BF), V((topk, tok_n), F32),
            V((tok_n, D), F32), V((topk, tok_n), F32),
            V((slots, D // 2), BF), V((2, slots, FF), BF), V((slots // 2, D), BF),
            pltpu.SemaphoreType.DMA((3,)),
            pltpu.SemaphoreType.DMA((8, 25)), pltpu.SemaphoreType.DMA((8, 25)),
            pltpu.SemaphoreType.DMA((16,)), pltpu.SemaphoreType.DMA((16,)),
        ],
        compiler_params=pltpu.CompilerParams(
            collective_id=0, has_side_effects=True, vmem_limit_bytes=57 * 2**20
        ),
        cost_estimate=pl.CostEstimate(
            flops=18 * slots * D * FF, bytes_accessed=20 * 2**20, transcendentals=2 * slots * FF
        ),
        name="moe",
    )(ids, probs, tokens, out_grad, triu, u, v, w_gate[0], w_up[0], w_down[0])
    lay, inp, prb, gate, up, down = pl.pallas_call(
        hand_over,
        out_shape=[sds(o.shape, o.dtype) for o in out[:6]],
        in_specs=[vm] * 6,
        out_specs=[hbm] * 6,
        scratch_shapes=[pltpu.SemaphoreType.DMA((6,))],
        compiler_params=pltpu.CompilerParams(vmem_limit_bytes=2**20),
        name="hand_over",
    )(*[pltpu.with_memory_space_constraint(o, pltpu.VMEM) for o in out[:6]])
    return lay, inp, prb.T, gate[None], up[None], down[None]


def solution(mesh):
    return jax.shard_map(
        per_device,
        mesh=mesh,
        in_specs=(
            P(("dp", "expert"), None),
            P(("dp", "expert"), None),
            P(("dp", "expert"), None),
            P(("dp", "expert"), None),
            P("expert", None, None),
            P("expert", None, None),
            P("expert", None, None),
        ),
        out_specs=(
            P(("dp", "expert"), None),
            P(("dp", "expert"), None),
            P(("dp", "expert"), None),
            P("expert", "dp", None),
            P("expert", "dp", None),
            P("expert", None, "dp"),
        ),
        check_vma=False,
    )
```

```python
import functools

import jax
import jax.numpy as jnp
import numpy as np
from jax import lax
from jax.experimental import pallas as pl
from jax.experimental.pallas import tpu as pltpu
from jax.sharding import PartitionSpec as P

MESH = pl.DeviceIdType.MESH
BF = jnp.bfloat16
F32 = jnp.float32

CAP = 12
ROWS = 16
T0, T1, G0, G1, O0, O1, R0, R1 = range(8)
SEND = {T0: 0, T1: 1, G0: 2, G1: 3, O0: 0, O1: 1, R0: 2, R1: 3}


def dot(a, b):
    return jnp.dot(a, b, preferred_element_type=F32)


def dot_nt(a, b):
    return lax.dot_general(a, b, (((1,), (1,)), ((), ())), preferred_element_type=F32)


def dot_tn(a, b):
    return lax.dot_general(a, b, (((0,), (0,)), ((), ())), preferred_element_type=F32)


def kernel(
    ids_ref, probs_ref, tok_ref, grad_ref, triu_ref, umat_ref, vmat_ref, wg_hbm, wu_hbm, wd_hbm,
    lay_out, inp_out, prb_out, gate_out, up_out, down_out, mid,
    send, recv, wg, wu, wd, rows, grads, act, hidden, pre, wide,
    ztok, zgrad, zids, zprobs, zlay_s, zinp_s, zprb_s, zlay_r, zinp_r, zprb_r,
    lay_acc, prb_acc, dprows, dppre, dpdown,
    wsem, ssem, rsem, xs, xr,
):
    tok_n, D = tok_ref.shape
    FF = wg.shape[1]
    Q = D // 4
    HALF = D // 2
    NB = recv.shape[2] * recv.shape[3] * 2
    GR = NB * CAP
    CR = GR // 2

    d = lax.axis_index("dp")
    e = lax.axis_index("expert")
    c = e % 2
    x = (e // 2) % 4
    zh = (e // 8) % 2
    y = e // 16

    def at(dp, yy, zz, xx, cc):
        return (dp, ((yy * 2 + zz) * 4 + xx) * 2 + cc)

    def px(k, dc):
        return at(d, y, zh, (x + k) % 4, (c + dc) % 2)

    def py(k, dc):
        return at(d, (y + k) % 4, zh, x, (c + dc) % 2)

    pz = at(1 - d, y, 1 - zh, x, c)
    pdp = (1 - d, e)
    pcore = at(d, y, zh, x, 1 - c)

    barrier = pltpu.get_barrier_semaphore()
    peers = [px(k, dc) for k in (1, 2, 3) for dc in (0, 1)]
    peers += [py(k, dc) for k in (1, 2, 3) for dc in (0, 1)]
    peers += [pz, pdp, pcore]
    for p in peers:
        pl.semaphore_signal(barrier, inc=1, device_id=p, device_id_type=MESH)

    weights = [
        pltpu.make_async_copy(src, dst, wsem.at[i])
        for i, (src, dst) in enumerate(((wg_hbm, wg), (wu_hbm, wu), (wd_hbm, wd)))
    ]
    for cp in weights:
        cp.start()

    def remote(src, dst, ss, rs, to):
        cp = pltpu.make_async_remote_copy(
            src_ref=src, dst_ref=dst, send_sem=ss, recv_sem=rs, device_id=to, device_id_type=MESH
        )
        cp.start()
        return cp

    count = [0]
    extras = []

    def extra(src, dst, to):
        i = count[0]
        count[0] += 1
        cp = remote(src, dst, xs.at[i], xr.at[i], to)
        extras.append(cp)
        return cp

    firsts, finals = {}, {}

    def first_legs(b):
        s = SEND[b]
        mids, ends = [], []
        n = 0
        for k in (1, 3, 2):
            for dc in (0, 1):
                to = px(k, 0) if dc == 0 else py(k, 1)
                mids.append(remote(
                    send.at[s, dc, k, pl.ds(1, 3)], mid.at[b, dc, k - 1],
                    ssem.at[b, n], rsem.at[b, n], to,
                ))
                n += 1
        for k in (1, 3, 2):
            for dc in (0, 1):
                to = px(k, 0) if dc == 0 else py(k, 1)
                ends.append(remote(
                    send.at[s, dc, k, 0], recv.at[b, dc, k, 0],
                    ssem.at[b, n], rsem.at[b, n], to,
                ))
                n += 1
                to = py(k, 0) if dc == 0 else px(k, 1)
                ends.append(remote(
                    send.at[s, dc, 0, k], recv.at[b, dc, 0, k],
                    ssem.at[b, n], rsem.at[b, n], to,
                ))
                n += 1
        ends.append(remote(
            send.at[s, 1, 0, 0], recv.at[b, 1, 0, 0], ssem.at[b, n], rsem.at[b, n], pcore,
        ))
        recv[b, 0, 0, 0] = send[s, 0, 0, 0]
        firsts[b] = (mids, ends)

    def second_legs(b):
        mids, ends = firsts[b]
        for cp in mids:
            cp.wait_recv()
        n = 19
        seconds = []
        for k in (1, 3, 2):
            for dc in (0, 1):
                to = py(k, 0) if dc == 0 else px(k, 0)
                seconds.append(remote(
                    mid.at[b, dc, pl.ds(0, 3), k - 1], recv.at[b, dc, pl.ds(1, 3), k],
                    ssem.at[b, n], rsem.at[b, n], to,
                ))
                n += 1
        finals[b] = ends + seconds

    def arrived(b):
        for cp in finals[b]:
            cp.wait_recv()

    sent = set()

    def sent_first(b):
        for cp in firsts[b][0] + firsts[b][1]:
            cp.wait_send()
        sent.add(b)

    def route(ids, probs, sign):
        b = lax.broadcasted_iota(jnp.int32, (NB, tok_n), 0)
        dc = b >> 4
        k1 = (b >> 2) & 3
        k2 = b & 3
        dx = jnp.where(dc == 0, k1, k2)
        dy = jnp.where(dc == 0, k2, k1)
        ee = ((((y + sign * dy) & 3) * 2 + zh) * 4 + ((x + sign * dx) & 3)) * 2 + ((c + dc) & 1)
        named = jnp.zeros((NB, tok_n), F32)
        prob = jnp.zeros((NB, tok_n), F32)
        for k in range(4):
            hit = ids[k : k + 1, :] == ee
            named = named + jnp.where(hit, 1.0, 0.0)
            prob = prob + jnp.where(hit, probs[k : k + 1, :], 0.0)
        rank = dot(named.astype(BF), triu_ref[...])
        pos = jnp.where(named > 0.0, rank, -100.0).astype(jnp.int32)
        return ee, pos, prob

    def slots(pos):
        shape = (NB, ROWS, tok_n)
        i = lax.broadcasted_iota(jnp.int32, shape, 1)
        at_pos = jnp.broadcast_to(pos[:, None, :], shape)
        main = at_pos == i
        ext = [at_pos == (i - CAP) * 3 + s for s in range(3)]
        return main, ext

    def flat(v):
        return v.reshape(NB * ROWS, tok_n)

    def ones(mask):
        return flat(jnp.where(mask, 1.0, 0.0)).astype(BF)

    def weighted(mask, prob):
        v = flat(jnp.where(mask, jnp.broadcast_to(prob[:, None, :], mask.shape), 0.0))
        hi = v.astype(BF)
        return hi, (v - hi.astype(F32)).astype(BF)

    def seg(s):
        return pl.ds(s * Q, Q)

    def pack_tokens(b, route_of, src):
        _, pos, _ = route_of
        main, ext = slots(pos)
        main = ones(main)
        for s in range(3):
            lhs = jnp.concatenate([main, ones(ext[s])], 1)
            rhs = jnp.concatenate([src[:, seg(s)], src[:, seg(3)]], 0)
            send[SEND[b], :, :, :, :, seg(s)] = dot(lhs, rhs).astype(BF).reshape(2, 4, 4, ROWS, Q)

    def pack_grads(b, route_of, src):
        _, pos, prob = route_of
        main, ext = slots(pos)
        main_hi, main_lo = weighted(main, prob)
        for s in range(3):
            ext_hi, ext_lo = weighted(ext[s], prob)
            lhs = jnp.concatenate([main_hi, ext_hi, main_lo, ext_lo], 1)
            rhs = jnp.concatenate([src[:, seg(s)], src[:, seg(3)]], 0)
            rhs = jnp.concatenate([rhs, rhs], 0)
            send[SEND[b], :, :, :, :, seg(s)] = dot(lhs, rhs).astype(BF).reshape(2, 4, 4, ROWS, Q)

    def unpack(b, put, w):
        for dc in range(2):
            r = pl.ds(w * GR + dc * CR, CR)
            last = jnp.zeros((CR, Q), F32)
            for s in range(3):
                piece = recv[b, dc, :, :, :, seg(s)].reshape(16 * ROWS, Q)
                put(r, s, dot(umat_ref[0], piece).astype(BF))
                last = last + dot(umat_ref[s + 1], piece)
            put(r, 3, last.astype(BF))

    def put_rows(r, s, value):
        rows[s // 2, r, pl.ds(s % 2 * Q, Q)] = value

    def put_grads(r, s, value):
        grads[r, seg(s)] = value

    def pack_rows(b):
        for dc in range(2):
            r = pl.ds(dc * CR, CR)
            for s in range(3):
                piece = dot(vmat_ref[0], wide[r, seg(s)]) + dot(vmat_ref[s + 1], wide[r, seg(3)])
                send[SEND[b], dc, :, :, :, seg(s)] = piece.astype(BF).reshape(4, 4, ROWS, Q)

    TF = 256

    def forward(w):
        r = pl.ds(w * GR, GR)

        @pl.loop(0, FF // TF)
        def _(n):
            col = pl.ds(pl.multiple_of(n * TF, TF), TF)
            lo, hi = pl.ds(0, HALF), pl.ds(HALF, HALF)
            ag = dot(rows[0, r, :], wg[lo, col]) + dot(rows[1, r, :], wg[hi, col])
            au = dot(rows[0, r, :], wu[lo, col]) + dot(rows[1, r, :], wu[hi, col])
            act[0, r, col] = ag
            act[1, r, col] = au
            hidden[r, col] = (ag * (1.0 / (1.0 + jnp.exp(-ag))) * au).astype(BF)

    def forward_out(w, b):
        r = pl.ds(w * GR, GR)

        @pl.loop(0, D // Q)
        def _(n):
            col = pl.ds(pl.multiple_of(n * Q, Q), Q)
            wide[:, col] = dot(hidden[r, :], wd[:, col]).astype(BF)

        pack_rows(b)

    def backward(w):
        r = pl.ds(w * GR, GR)

        @pl.loop(0, FF // TF)
        def _(n):
            col = pl.ds(pl.multiple_of(n * TF, TF), TF)
            hg = dot_nt(grads[r, :], wd[col, :])
            ag = act[0, r, col]
            s = 1.0 / (1.0 + jnp.exp(-ag))
            pre[0, r, col] = (hg * act[1, r, col] * s * (1.0 + ag * (1.0 - s))).astype(BF)
            pre[1, r, col] = (hg * (ag * s)).astype(BF)

    def backward_rows(w, b):
        r = pl.ds(w * GR, GR)

        @pl.loop(0, D // TF)
        def _(n):
            col = pl.ds(pl.multiple_of(n * TF, TF), TF)
            total = dot_nt(pre[0, r, :], wg[col, :]) + dot_nt(pre[1, r, :], wu[col, :])
            wide[:, col] = total.astype(BF)

        pack_rows(b)

    def combine_out(b, route_of, ids, g_ref, lay, prb):
        ee, pos, prob = route_of
        main, ext = slots(pos)
        main_hi, main_lo = weighted(main, prob)
        main_m = flat(jnp.where(main, 1.0, 0.0))
        last = jnp.zeros((tok_n, Q), F32)
        inner = jnp.zeros((NB * ROWS, tok_n), F32)
        for s in range(3):
            ext_hi, ext_lo = weighted(ext[s], prob)
            piece = recv[b, :, :, :, :, seg(s)].reshape(NB * ROWS, Q)
            both = dot_tn(jnp.concatenate([main_hi, ext_hi], 1), piece)
            both = both + dot_tn(jnp.concatenate([main_lo, ext_lo], 1), piece)
            lay[:, seg(s)] = both[:tok_n].astype(lay.dtype)
            last = last + both[tok_n:]
            ext_m = flat(jnp.where(ext[s], 1.0, 0.0))
            inner = inner + dot_nt(piece, g_ref[:, seg(s)]) * main_m
            inner = inner + dot_nt(piece, g_ref[:, seg(3)]) * ext_m
        lay[:, seg(3)] = last.astype(lay.dtype)
        inner = jnp.sum(inner.reshape(NB, ROWS, tok_n), 1)
        for k in range(4):
            hit = ids[k : k + 1, :] == ee
            prb[k : k + 1, :] = jnp.sum(jnp.where(hit, inner, 0.0), 0, keepdims=True)

    def sum_matrices(route_of):
        main, ext = slots(route_of[1])
        main = ones(main)
        return [jnp.concatenate([main, ones(ext[s])], 1) for s in range(3)]

    def combine_grad(b, sums, dst):
        last = jnp.zeros((tok_n, Q), F32)
        for s in range(3):
            piece = recv[b, :, :, :, :, seg(s)].reshape(NB * ROWS, Q)
            both = dot_tn(sums[s], piece)
            dst[:, seg(s)] = both[:tok_n].astype(dst.dtype)
            last = last + both[tok_n:]
        dst[:, seg(3)] = last.astype(dst.dtype)

    mine = pl.multiple_of(d * HALF, HALF)
    other = pl.multiple_of((1 - d) * HALF, HALF)

    def dp_rows(w):
        r = pl.ds(w * GR, GR)
        return extra(rows.at[1 - d, r], dprows.at[r], pdp)

    def dp_pre(w):
        r = pl.ds(w * GR, GR)
        return [extra(pre.at[i, r], dppre.at[i, r], pdp) for i in range(2)]

    FB = FF // 2

    def down_part(n, half):
        return dot_tn(hidden[:, pl.ds(n * FB, FB)], grads[:, pl.ds(half, HALF)])

    own_ids, own_probs = ids_ref[...], probs_ref[...]
    to_own = route(own_ids, own_probs, 1)
    pack_tokens(T0, to_own, tok_ref)
    pl.semaphore_wait(barrier, len(peers))
    z_ids = extra(ids_ref, zids, pz)
    z_probs = extra(probs_ref, zprobs, pz)
    z_tok = extra(tok_ref, ztok, pz)
    first_legs(T0)
    pack_grads(G0, to_own, grad_ref)
    z_ids.wait_recv()
    z_probs.wait_recv()
    z_ids_v, z_probs_v = zids[...], zprobs[...]
    to_z = route(z_ids_v, z_probs_v, 1)
    second_legs(T0)
    z_tok.wait_recv()
    z_grad = extra(grad_ref, zgrad, pz)
    pack_tokens(T1, to_z, ztok)
    first_legs(T1)
    for cp in weights:
        cp.wait()
    arrived(T0)
    unpack(T0, put_rows, 0)
    dp_in = [dp_rows(0)]
    second_legs(T1)
    first_legs(G0)
    forward(0)
    sent_first(T0)
    forward_out(0, O0)
    z_grad.wait_recv()
    pack_grads(G1, to_z, zgrad)
    second_legs(G0)
    first_legs(G1)
    arrived(T1)
    unpack(T1, put_rows, 1)
    dp_in.append(dp_rows(1))
    forward(1)
    sent_first(T1)
    forward_out(1, O1)
    arrived(G0)
    unpack(G0, put_grads, 0)
    backward(0)
    dp_in += dp_pre(0)
    second_legs(G1)
    first_legs(O0)
    sent_first(G0)
    backward_rows(0, R0)
    first_legs(O1)
    arrived(G1)
    unpack(G1, put_grads, 1)
    backward(1)
    dp_in += dp_pre(1)
    second_legs(O0)
    sent_first(G1)
    backward_rows(1, R1)
    first_legs(R1)
    for n in range(2):
        wide[:, pl.ds(n * HALF, HALF)] = down_part(n, other).astype(BF)
    dp_down = extra(wide, dpdown, pdp)
    second_legs(O1)
    first_legs(R0)
    for n in range(2):
        own = down_part(n, mine)
        act[n, pl.ds(0, FB), :] = own[:, :FF]
        act[n, pl.ds(FB, FB), pl.ds(0, HALF - FF)] = own[:, FF:]
    second_legs(R1)
    own_back = route(own_ids, own_probs, -1)
    z_back = route(z_ids_v, z_probs_v, -1)
    arrived(O1)
    combine_out(O1, z_back, z_ids_v, zgrad, zlay_s, zprb_s)
    z_lay = extra(zlay_s, zlay_r, pz)
    z_prb = extra(zprb_s, zprb_r, pz)
    arrived(O0)
    combine_out(O0, own_back, own_ids, grad_ref, lay_acc, prb_acc)
    second_legs(R0)
    z_sums = sum_matrices(z_back)
    arrived(R1)
    combine_grad(R1, z_sums, zinp_s)
    z_inp = extra(zinp_s, zinp_r, pz)
    z_lay.wait_recv()
    lay_out[...] = (lay_acc[...] + zlay_r[...].astype(F32)).astype(BF)
    z_prb.wait_recv()
    prb_out[...] = prb_acc[...] + zprb_r[...]

    for cp in dp_in:
        cp.wait_recv()

    TG = 256

    @pl.loop(0, HALF // TG)
    def _(n):
        at_n = pl.multiple_of(n * TG, TG)
        own = rows[d, :, pl.ds(at_n, TG)]
        theirs = dprows[:, pl.ds(at_n, TG)]
        for i, out in enumerate((gate_out, up_out)):
            total = dot_tn(own, pre[i]) + dot_tn(theirs, dppre[i])
            out[pl.ds(at_n, TG), :] = total.astype(BF)

    own_sums = sum_matrices(own_back)
    arrived(R0)
    combine_grad(R0, own_sums, lay_acc)
    z_inp.wait_recv()
    inp_out[...] = (lay_acc[...] + zinp_r[...].astype(F32)).astype(BF)

    dp_down.wait_recv()
    for n in range(2):
        theirs = dpdown[:, pl.ds(n * HALF, HALF)].astype(F32)
        r = pl.ds(n * FB, FB)
        down_out[r, pl.ds(0, FF)] = (act[n, pl.ds(0, FB), :] + theirs[:, :FF]).astype(BF)
        own = act[n, pl.ds(FB, FB), pl.ds(0, HALF - FF)]
        down_out[r, pl.ds(FF, HALF - FF)] = (own + theirs[:, FF:]).astype(BF)
    for b in range(8):
        if b not in sent:
            sent_first(b)
        for cp in finals[b][len(firsts[b][1]) :]:
            cp.wait_send()
    for cp in extras:
        cp.wait_send()


def hand_over(*refs):
    sem = refs[12]
    copies = [pltpu.make_async_copy(refs[i], refs[6 + i], sem.at[i]) for i in range(6)]
    for cp in copies:
        cp.start()
    for cp in copies:
        cp.wait()


def matrices():
    u = np.zeros((4, 16, CAP, 16, ROWS), np.float32)
    v = np.zeros((4, 16, ROWS, 16, CAP), np.float32)
    for k in range(16):
        m = ((4 - k // 4) % 4) * 4 + (4 - k % 4) % 4
        for i in range(CAP):
            u[0, k, i, k, i] = 1
            v[0, m, i, k, i] = 1
            u[1 + i % 3, k, i, k, CAP + i // 3] = 1
            v[1 + i % 3, m, CAP + i // 3, k, i] = 1
    u = u.reshape(4, 16 * CAP, 16 * ROWS)
    v = v.reshape(4, 16 * ROWS, 16 * CAP)
    return jnp.asarray(u, BF), jnp.asarray(v, BF)


def per_device(tokens, out_grad, expert_ids, gate_probs, w_gate, w_up, w_down):
    tok_n, D = tokens.shape
    topk = expert_ids.shape[1]
    FF = w_gate.shape[2]
    W = 3 * D // 4
    slots = 64 * CAP
    ids, probs = expert_ids.T, gate_probs.T
    triu = jnp.asarray(np.triu(np.ones((tok_n, tok_n), np.float32), 1), BF)
    u, v = matrices()
    vm = pl.BlockSpec(memory_space=pltpu.VMEM)
    hbm = pl.BlockSpec(memory_space=pl.ANY)
    sds = jax.ShapeDtypeStruct
    V = pltpu.VMEM
    out = pl.pallas_call(
        kernel,
        out_shape=(
            V((tok_n, D), BF), V((tok_n, D), BF), V((topk, tok_n), F32),
            V((D // 2, FF), BF), V((D // 2, FF), BF), V((FF, D // 2), BF),
            sds((8, 2, 3, 3, ROWS, W), BF),
        ),
        in_specs=[vm] * 7 + [hbm] * 3,
        out_specs=(vm,) * 6 + (hbm,),
        scratch_shapes=[
            V((4, 2, 4, 4, ROWS, W), BF), V((8, 2, 4, 4, ROWS, W), BF),
            V((D, FF), BF), V((D, FF), BF), V((FF, D), BF),
            V((2, slots, D // 2), BF), V((slots, D), BF),
            V((2, slots, FF), F32), V((slots, FF), BF), V((2, slots, FF), BF),
            V((slots // 2, D), BF),
            V((tok_n, D), BF), V((tok_n, D), BF), V((topk, tok_n), jnp.int32), V((topk, tok_n), F32),
            V((tok_n, D), BF), V((tok_n, D), BF), V((topk, tok_n), F32),
            V((tok_n, D), BF), V((tok_n, D), BF), V((topk, tok_n), F32),
            V((tok_n, D), F32), V((topk, tok_n), F32),
            V((slots, D // 2), BF), V((2, slots, FF), BF), V((slots // 2, D), BF),
            pltpu.SemaphoreType.DMA((3,)),
            pltpu.SemaphoreType.DMA((8, 25)), pltpu.SemaphoreType.DMA((8, 25)),
            pltpu.SemaphoreType.DMA((16,)), pltpu.SemaphoreType.DMA((16,)),
        ],
        compiler_params=pltpu.CompilerParams(
            collective_id=0, has_side_effects=True, vmem_limit_bytes=57 * 2**20
        ),
        cost_estimate=pl.CostEstimate(
            flops=18 * slots * D * FF, bytes_accessed=20 * 2**20, transcendentals=2 * slots * FF
        ),
        name="moe",
    )(ids, probs, tokens, out_grad, triu, u, v, w_gate[0], w_up[0], w_down[0])
    lay, inp, prb, gate, up, down = pl.pallas_call(
        hand_over,
        out_shape=[sds(o.shape, o.dtype) for o in out[:6]],
        in_specs=[vm] * 6,
        out_specs=[hbm] * 6,
        scratch_shapes=[pltpu.SemaphoreType.DMA((6,))],
        compiler_params=pltpu.CompilerParams(vmem_limit_bytes=2**20),
        name="hand_over",
    )(*[pltpu.with_memory_space_constraint(o, pltpu.VMEM) for o in out[:6]])
    return lay, inp, prb.T, gate[None], up[None], down[None]


def solution(mesh):
    return jax.shard_map(
        per_device,
        mesh=mesh,
        in_specs=(
            P(("dp", "expert"), None),
            P(("dp", "expert"), None),
            P(("dp", "expert"), None),
            P(("dp", "expert"), None),
            P("expert", None, None),
            P("expert", None, None),
            P("expert", None, None),
        ),
        out_specs=(
            P(("dp", "expert"), None),
            P(("dp", "expert"), None),
            P(("dp", "expert"), None),
            P("expert", "dp", None),
            P("expert", "dp", None),
            P("expert", None, "dp"),
        ),
        check_vma=False,
    )
```

```python
import functools

import jax
import jax.numpy as jnp
import numpy as np
from jax import lax
from jax.experimental import pallas as pl
from jax.experimental.pallas import tpu as pltpu
from jax.sharding import PartitionSpec as P

MESH = pl.DeviceIdType.MESH
BF = jnp.bfloat16
F32 = jnp.float32

CAP = 12
ROWS = 16
T0, T1, G0, G1, O0, O1, R0, R1 = range(8)
SEND = {T0: 0, T1: 1, G0: 2, G1: 3, O0: 0, O1: 1, R0: 2, R1: 3}


def dot(a, b):
    return jnp.dot(a, b, preferred_element_type=F32)


def dot_nt(a, b):
    return lax.dot_general(a, b, (((1,), (1,)), ((), ())), preferred_element_type=F32)


def dot_tn(a, b):
    return lax.dot_general(a, b, (((0,), (0,)), ((), ())), preferred_element_type=F32)


def kernel(
    ids_ref, probs_ref, tok_ref, grad_ref, triu_ref, umat_ref, vmat_ref, wg_hbm, wu_hbm, wd_hbm,
    lay_out, inp_out, prb_out, gate_out, up_out, down_out, mid,
    send, recv, wg, wu, wd, rows, grads, act, hidden, pre, wide,
    ztok, zgrad, zids, zprobs, zlay_s, zinp_s, zprb_s, zlay_r, zinp_r, zprb_r,
    lay_acc, prb_acc, dprows, dppre, dpdown,
    wsem, ssem, rsem, xs, xr,
):
    tok_n, D = tok_ref.shape
    FF = wg.shape[1]
    Q = D // 4
    HALF = D // 2
    NB = recv.shape[2] * recv.shape[3] * 2
    GR = NB * CAP
    CR = GR // 2

    d = lax.axis_index("dp")
    e = lax.axis_index("expert")
    c = e % 2
    x = (e // 2) % 4
    zh = (e // 8) % 2
    y = e // 16

    def at(dp, yy, zz, xx, cc):
        return (dp, ((yy * 2 + zz) * 4 + xx) * 2 + cc)

    def px(k, dc):
        return at(d, y, zh, (x + k) % 4, (c + dc) % 2)

    def py(k, dc):
        return at(d, (y + k) % 4, zh, x, (c + dc) % 2)

    pz = at(1 - d, y, 1 - zh, x, c)
    pdp = (1 - d, e)
    pcore = at(d, y, zh, x, 1 - c)

    barrier = pltpu.get_barrier_semaphore()
    peers = [px(k, dc) for k in (1, 2, 3) for dc in (0, 1)]
    peers += [py(k, dc) for k in (1, 2, 3) for dc in (0, 1)]
    peers += [pz, pdp, pcore]
    for p in peers:
        pl.semaphore_signal(barrier, inc=1, device_id=p, device_id_type=MESH)

    weights = [
        pltpu.make_async_copy(src, dst, wsem.at[i])
        for i, (src, dst) in enumerate(((wg_hbm, wg), (wu_hbm, wu), (wd_hbm, wd)))
    ]
    for cp in weights:
        cp.start()

    def remote(src, dst, ss, rs, to):
        cp = pltpu.make_async_remote_copy(
            src_ref=src, dst_ref=dst, send_sem=ss, recv_sem=rs, device_id=to, device_id_type=MESH
        )
        cp.start()
        return cp

    count = [0]
    extras = []

    def extra(src, dst, to):
        i = count[0]
        count[0] += 1
        cp = remote(src, dst, xs.at[i], xr.at[i], to)
        extras.append(cp)
        return cp

    firsts, finals = {}, {}

    def first_legs(b):
        s = SEND[b]
        mids, ends = [], []
        n = 0
        for k in (2, 1, 3):
            for dc in (0, 1):
                to = px(k, 0) if dc == 0 else py(k, 1)
                mids.append(remote(
                    send.at[s, dc, k, pl.ds(1, 3)], mid.at[b, dc, k - 1],
                    ssem.at[b, n], rsem.at[b, n], to,
                ))
                n += 1
        for k in (2, 1, 3):
            for dc in (0, 1):
                to = px(k, 0) if dc == 0 else py(k, 1)
                ends.append(remote(
                    send.at[s, dc, k, 0], recv.at[b, dc, k, 0],
                    ssem.at[b, n], rsem.at[b, n], to,
                ))
                n += 1
                to = py(k, 0) if dc == 0 else px(k, 1)
                ends.append(remote(
                    send.at[s, dc, 0, k], recv.at[b, dc, 0, k],
                    ssem.at[b, n], rsem.at[b, n], to,
                ))
                n += 1
        ends.append(remote(
            send.at[s, 1, 0, 0], recv.at[b, 1, 0, 0], ssem.at[b, n], rsem.at[b, n], pcore,
        ))
        recv[b, 0, 0, 0] = send[s, 0, 0, 0]
        firsts[b] = (mids, ends)

    def second_legs(b):
        mids, ends = firsts[b]
        for cp in mids:
            cp.wait_recv()
        n = 19
        seconds = []
        for k in (2, 1, 3):
            for dc in (0, 1):
                to = py(k, 0) if dc == 0 else px(k, 0)
                seconds.append(remote(
                    mid.at[b, dc, pl.ds(0, 3), k - 1], recv.at[b, dc, pl.ds(1, 3), k],
                    ssem.at[b, n], rsem.at[b, n], to,
                ))
                n += 1
        finals[b] = ends + seconds

    def arrived(b):
        for cp in finals[b]:
            cp.wait_recv()

    sent = set()

    def sent_first(b):
        for cp in firsts[b][0] + firsts[b][1]:
            cp.wait_send()
        sent.add(b)

    def route(ids, probs, sign):
        b = lax.broadcasted_iota(jnp.int32, (NB, tok_n), 0)
        dc = b >> 4
        k1 = (b >> 2) & 3
        k2 = b & 3
        dx = jnp.where(dc == 0, k1, k2)
        dy = jnp.where(dc == 0, k2, k1)
        ee = ((((y + sign * dy) & 3) * 2 + zh) * 4 + ((x + sign * dx) & 3)) * 2 + ((c + dc) & 1)
        named = jnp.zeros((NB, tok_n), F32)
        prob = jnp.zeros((NB, tok_n), F32)
        for k in range(4):
            hit = ids[k : k + 1, :] == ee
            named = named + jnp.where(hit, 1.0, 0.0)
            prob = prob + jnp.where(hit, probs[k : k + 1, :], 0.0)
        rank = dot(named.astype(BF), triu_ref[...])
        pos = jnp.where(named > 0.0, rank, -100.0).astype(jnp.int32)
        return ee, pos, prob

    def slots(pos):
        shape = (NB, ROWS, tok_n)
        i = lax.broadcasted_iota(jnp.int32, shape, 1)
        at_pos = jnp.broadcast_to(pos[:, None, :], shape)
        main = at_pos == i
        ext = [at_pos == (i - CAP) * 3 + s for s in range(3)]
        return main, ext

    def flat(v):
        return v.reshape(NB * ROWS, tok_n)

    def ones(mask):
        return flat(jnp.where(mask, 1.0, 0.0)).astype(BF)

    def weighted(mask, prob):
        v = flat(jnp.where(mask, jnp.broadcast_to(prob[:, None, :], mask.shape), 0.0))
        hi = v.astype(BF)
        return hi, (v - hi.astype(F32)).astype(BF)

    def seg(s):
        return pl.ds(s * Q, Q)

    def pack_tokens(b, route_of, src):
        _, pos, _ = route_of
        main, ext = slots(pos)
        main = ones(main)
        for s in range(3):
            lhs = jnp.concatenate([main, ones(ext[s])], 1)
            rhs = jnp.concatenate([src[:, seg(s)], src[:, seg(3)]], 0)
            send[SEND[b], :, :, :, :, seg(s)] = dot(lhs, rhs).astype(BF).reshape(2, 4, 4, ROWS, Q)

    def pack_grads(b, route_of, src):
        _, pos, prob = route_of
        main, ext = slots(pos)
        main_hi, main_lo = weighted(main, prob)
        for s in range(3):
            ext_hi, ext_lo = weighted(ext[s], prob)
            lhs = jnp.concatenate([main_hi, ext_hi, main_lo, ext_lo], 1)
            rhs = jnp.concatenate([src[:, seg(s)], src[:, seg(3)]], 0)
            rhs = jnp.concatenate([rhs, rhs], 0)
            send[SEND[b], :, :, :, :, seg(s)] = dot(lhs, rhs).astype(BF).reshape(2, 4, 4, ROWS, Q)

    def unpack(b, put, w, classes=(0, 1)):
        for dc in classes:
            r = pl.ds(w * GR + dc * CR, CR)
            last = jnp.zeros((CR, Q), F32)
            for s in range(3):
                piece = recv[b, dc, :, :, :, seg(s)].reshape(16 * ROWS, Q)
                put(r, s, dot(umat_ref[0], piece).astype(BF))
                last = last + dot(umat_ref[s + 1], piece)
            put(r, 3, last.astype(BF))

    def put_rows(r, s, value):
        rows[s // 2, r, pl.ds(s % 2 * Q, Q)] = value

    def put_grads(r, s, value):
        grads[r, seg(s)] = value

    def pack_rows(b):
        for dc in range(2):
            r = pl.ds(dc * CR, CR)
            for s in range(3):
                piece = dot(vmat_ref[0], wide[r, seg(s)]) + dot(vmat_ref[s + 1], wide[r, seg(3)])
                send[SEND[b], dc, :, :, :, seg(s)] = piece.astype(BF).reshape(4, 4, ROWS, Q)

    TF = 256

    def forward(w):
        r = pl.ds(w * GR, GR)

        @pl.loop(0, FF // TF)
        def _(n):
            col = pl.ds(pl.multiple_of(n * TF, TF), TF)
            lo, hi = pl.ds(0, HALF), pl.ds(HALF, HALF)
            ag = dot(rows[0, r, :], wg[lo, col]) + dot(rows[1, r, :], wg[hi, col])
            au = dot(rows[0, r, :], wu[lo, col]) + dot(rows[1, r, :], wu[hi, col])
            act[0, r, col] = ag
            act[1, r, col] = au
            hidden[r, col] = (ag * (1.0 / (1.0 + jnp.exp(-ag))) * au).astype(BF)

    def forward_out(w, b):
        r = pl.ds(w * GR, GR)

        @pl.loop(0, D // Q)
        def _(n):
            col = pl.ds(pl.multiple_of(n * Q, Q), Q)
            wide[:, col] = dot(hidden[r, :], wd[:, col]).astype(BF)

        pack_rows(b)

    def backward(r):
        @pl.loop(0, FF // TF)
        def _(n):
            col = pl.ds(pl.multiple_of(n * TF, TF), TF)
            hg = dot_nt(grads[r, :], wd[col, :])
            ag = act[0, r, col]
            s = 1.0 / (1.0 + jnp.exp(-ag))
            pre[0, r, col] = (hg * act[1, r, col] * s * (1.0 + ag * (1.0 - s))).astype(BF)
            pre[1, r, col] = (hg * (ag * s)).astype(BF)

    def backward_rows(w, b):
        r = pl.ds(w * GR, GR)

        @pl.loop(0, D // TF)
        def _(n):
            col = pl.ds(pl.multiple_of(n * TF, TF), TF)
            total = dot_nt(pre[0, r, :], wg[col, :]) + dot_nt(pre[1, r, :], wu[col, :])
            wide[:, col] = total.astype(BF)

        pack_rows(b)

    def combine_out(b, route_of, ids, g_ref, lay, prb):
        ee, pos, prob = route_of
        main, ext = slots(pos)
        main_hi, main_lo = weighted(main, prob)
        main_m = flat(jnp.where(main, 1.0, 0.0))
        last = jnp.zeros((tok_n, Q), F32)
        inner = jnp.zeros((NB * ROWS, tok_n), F32)
        for s in range(3):
            ext_hi, ext_lo = weighted(ext[s], prob)
            piece = recv[b, :, :, :, :, seg(s)].reshape(NB * ROWS, Q)
            both = dot_tn(jnp.concatenate([main_hi, ext_hi], 1), piece)
            both = both + dot_tn(jnp.concatenate([main_lo, ext_lo], 1), piece)
            lay[:, seg(s)] = both[:tok_n].astype(lay.dtype)
            last = last + both[tok_n:]
            ext_m = flat(jnp.where(ext[s], 1.0, 0.0))
            inner = inner + dot_nt(piece, g_ref[:, seg(s)]) * main_m
            inner = inner + dot_nt(piece, g_ref[:, seg(3)]) * ext_m
        lay[:, seg(3)] = last.astype(lay.dtype)
        inner = jnp.sum(inner.reshape(NB, ROWS, tok_n), 1)
        for k in range(4):
            hit = ids[k : k + 1, :] == ee
            prb[k : k + 1, :] = jnp.sum(jnp.where(hit, inner, 0.0), 0, keepdims=True)

    def sum_matrices(route_of):
        main, ext = slots(route_of[1])
        main = ones(main)
        return [jnp.concatenate([main, ones(ext[s])], 1) for s in range(3)]

    def combine_grad(b, sums, dst):
        last = jnp.zeros((tok_n, Q), F32)
        for s in range(3):
            piece = recv[b, :, :, :, :, seg(s)].reshape(NB * ROWS, Q)
            both = dot_tn(sums[s], piece)
            dst[:, seg(s)] = both[:tok_n].astype(dst.dtype)
            last = last + both[tok_n:]
        dst[:, seg(3)] = last.astype(dst.dtype)

    mine = pl.multiple_of(d * HALF, HALF)
    other = pl.multiple_of((1 - d) * HALF, HALF)

    def dp_rows(w):
        r = pl.ds(w * GR, GR)
        return extra(rows.at[1 - d, r], dprows.at[r], pdp)

    def dp_pre(r):
        return [extra(pre.at[i, r], dppre.at[i, r], pdp) for i in range(2)]

    FB = FF // 2

    def down_part(n, half):
        return dot_tn(hidden[:, pl.ds(n * FB, FB)], grads[:, pl.ds(half, HALF)])

    own_ids, own_probs = ids_ref[...], probs_ref[...]
    to_own = route(own_ids, own_probs, 1)
    pack_tokens(T0, to_own, tok_ref)
    pl.semaphore_wait(barrier, len(peers))
    z_ids = extra(ids_ref, zids, pz)
    z_probs = extra(probs_ref, zprobs, pz)
    z_tok = extra(tok_ref, ztok, pz)
    first_legs(T0)
    pack_grads(G0, to_own, grad_ref)
    z_ids.wait_recv()
    z_probs.wait_recv()
    z_ids_v, z_probs_v = zids[...], zprobs[...]
    to_z = route(z_ids_v, z_probs_v, 1)
    second_legs(T0)
    z_tok.wait_recv()
    z_grad = extra(grad_ref, zgrad, pz)
    pack_tokens(T1, to_z, ztok)
    first_legs(T1)
    for cp in weights:
        cp.wait()
    arrived(T0)
    unpack(T0, put_rows, 0)
    dp_in = [dp_rows(0)]
    second_legs(T1)
    first_legs(G0)
    forward(0)
    sent_first(T0)
    forward_out(0, O0)
    z_grad.wait_recv()
    pack_grads(G1, to_z, zgrad)
    second_legs(G0)
    first_legs(G1)
    arrived(T1)
    unpack(T1, put_rows, 1)
    dp_in.append(dp_rows(1))
    forward(1)
    sent_first(T1)
    forward_out(1, O1)
    arrived(G0)
    for dc in range(2):
        unpack(G0, put_grads, 0, (dc,))
        backward(pl.ds(dc * CR, CR))
        dp_in += dp_pre(pl.ds(dc * CR, CR))
    second_legs(G1)
    first_legs(O0)
    sent_first(G0)
    backward_rows(0, R0)
    arrived(G1)
    unpack(G1, put_grads, 1)
    backward(pl.ds(GR, GR))
    dp_in += dp_pre(pl.ds(GR, GR))
    second_legs(O0)
    first_legs(O1)
    sent_first(G1)
    backward_rows(1, R1)
    for n in range(2):
        wide[:, pl.ds(n * HALF, HALF)] = down_part(n, other).astype(BF)
    dp_down = extra(wide, dpdown, pdp)
    second_legs(O1)
    first_legs(R1)
    for n in range(2):
        own = down_part(n, mine)
        act[n, pl.ds(0, FB), :] = own[:, :FF]
        act[n, pl.ds(FB, FB), pl.ds(0, HALF - FF)] = own[:, FF:]
    second_legs(R1)
    first_legs(R0)
    own_back = route(own_ids, own_probs, -1)
    z_back = route(z_ids_v, z_probs_v, -1)
    arrived(O1)
    combine_out(O1, z_back, z_ids_v, zgrad, zlay_s, zprb_s)
    z_lay = extra(zlay_s, zlay_r, pz)
    z_prb = extra(zprb_s, zprb_r, pz)
    arrived(O0)
    combine_out(O0, own_back, own_ids, grad_ref, lay_acc, prb_acc)
    second_legs(R0)
    z_sums = sum_matrices(z_back)
    arrived(R1)
    combine_grad(R1, z_sums, zinp_s)
    z_inp = extra(zinp_s, zinp_r, pz)
    z_lay.wait_recv()
    lay_out[...] = (lay_acc[...] + zlay_r[...].astype(F32)).astype(BF)
    z_prb.wait_recv()
    prb_out[...] = prb_acc[...] + zprb_r[...]

    for cp in dp_in:
        cp.wait_recv()

    TG = 256

    @pl.loop(0, HALF // TG)
    def _(n):
        at_n = pl.multiple_of(n * TG, TG)
        own = rows[d, :, pl.ds(at_n, TG)]
        theirs = dprows[:, pl.ds(at_n, TG)]
        for i, out in enumerate((gate_out, up_out)):
            total = dot_tn(own, pre[i]) + dot_tn(theirs, dppre[i])
            out[pl.ds(at_n, TG), :] = total.astype(BF)

    own_sums = sum_matrices(own_back)
    arrived(R0)
    combine_grad(R0, own_sums, lay_acc)
    z_inp.wait_recv()
    inp_out[...] = (lay_acc[...] + zinp_r[...].astype(F32)).astype(BF)

    dp_down.wait_recv()
    for n in range(2):
        theirs = dpdown[:, pl.ds(n * HALF, HALF)].astype(F32)
        r = pl.ds(n * FB, FB)
        down_out[r, pl.ds(0, FF)] = (act[n, pl.ds(0, FB), :] + theirs[:, :FF]).astype(BF)
        own = act[n, pl.ds(FB, FB), pl.ds(0, HALF - FF)]
        down_out[r, pl.ds(FF, HALF - FF)] = (own + theirs[:, FF:]).astype(BF)
    for b in range(8):
        if b not in sent:
            sent_first(b)
        for cp in finals[b][len(firsts[b][1]) :]:
            cp.wait_send()
    for cp in extras:
        cp.wait_send()


def hand_over(*refs):
    sem = refs[12]
    copies = [pltpu.make_async_copy(refs[i], refs[6 + i], sem.at[i]) for i in range(6)]
    for cp in copies:
        cp.start()
    for cp in copies:
        cp.wait()


def matrices():
    u = np.zeros((4, 16, CAP, 16, ROWS), np.float32)
    v = np.zeros((4, 16, ROWS, 16, CAP), np.float32)
    for k in range(16):
        m = ((4 - k // 4) % 4) * 4 + (4 - k % 4) % 4
        for i in range(CAP):
            u[0, k, i, k, i] = 1
            v[0, m, i, k, i] = 1
            u[1 + i % 3, k, i, k, CAP + i // 3] = 1
            v[1 + i % 3, m, CAP + i // 3, k, i] = 1
    u = u.reshape(4, 16 * CAP, 16 * ROWS)
    v = v.reshape(4, 16 * ROWS, 16 * CAP)
    return jnp.asarray(u, BF), jnp.asarray(v, BF)


def per_device(tokens, out_grad, expert_ids, gate_probs, w_gate, w_up, w_down):
    tok_n, D = tokens.shape
    topk = expert_ids.shape[1]
    FF = w_gate.shape[2]
    W = 3 * D // 4
    slots = 64 * CAP
    ids, probs = expert_ids.T, gate_probs.T
    triu = jnp.asarray(np.triu(np.ones((tok_n, tok_n), np.float32), 1), BF)
    u, v = matrices()
    vm = pl.BlockSpec(memory_space=pltpu.VMEM)
    hbm = pl.BlockSpec(memory_space=pl.ANY)
    sds = jax.ShapeDtypeStruct
    V = pltpu.VMEM
    out = pl.pallas_call(
        kernel,
        out_shape=(
            V((tok_n, D), BF), V((tok_n, D), BF), V((topk, tok_n), F32),
            V((D // 2, FF), BF), V((D // 2, FF), BF), V((FF, D // 2), BF),
            sds((8, 2, 3, 3, ROWS, W), BF),
        ),
        in_specs=[vm] * 7 + [hbm] * 3,
        out_specs=(vm,) * 6 + (hbm,),
        scratch_shapes=[
            V((4, 2, 4, 4, ROWS, W), BF), V((8, 2, 4, 4, ROWS, W), BF),
            V((D, FF), BF), V((D, FF), BF), V((FF, D), BF),
            V((2, slots, D // 2), BF), V((slots, D), BF),
            V((2, slots, FF), F32), V((slots, FF), BF), V((2, slots, FF), BF),
            V((slots // 2, D), BF),
            V((tok_n, D), BF), V((tok_n, D), BF), V((topk, tok_n), jnp.int32), V((topk, tok_n), F32),
            V((tok_n, D), BF), V((tok_n, D), BF), V((topk, tok_n), F32),
            V((tok_n, D), BF), V((tok_n, D), BF), V((topk, tok_n), F32),
            V((tok_n, D), F32), V((topk, tok_n), F32),
            V((slots, D // 2), BF), V((2, slots, FF), BF), V((slots // 2, D), BF),
            pltpu.SemaphoreType.DMA((3,)),
            pltpu.SemaphoreType.DMA((8, 25)), pltpu.SemaphoreType.DMA((8, 25)),
            pltpu.SemaphoreType.DMA((16,)), pltpu.SemaphoreType.DMA((16,)),
        ],
        compiler_params=pltpu.CompilerParams(
            collective_id=0, has_side_effects=True, vmem_limit_bytes=57 * 2**20
        ),
        cost_estimate=pl.CostEstimate(
            flops=18 * slots * D * FF, bytes_accessed=20 * 2**20, transcendentals=2 * slots * FF
        ),
        name="moe",
    )(ids, probs, tokens, out_grad, triu, u, v, w_gate[0], w_up[0], w_down[0])
    lay, inp, prb, gate, up, down = pl.pallas_call(
        hand_over,
        out_shape=[sds(o.shape, o.dtype) for o in out[:6]],
        in_specs=[vm] * 6,
        out_specs=[hbm] * 6,
        scratch_shapes=[pltpu.SemaphoreType.DMA((6,))],
        compiler_params=pltpu.CompilerParams(vmem_limit_bytes=2**20),
        name="hand_over",
    )(*[pltpu.with_memory_space_constraint(o, pltpu.VMEM) for o in out[:6]])
    return lay, inp, prb.T, gate[None], up[None], down[None]


def solution(mesh):
    return jax.shard_map(
        per_device,
        mesh=mesh,
        in_specs=(
            P(("dp", "expert"), None),
            P(("dp", "expert"), None),
            P(("dp", "expert"), None),
            P(("dp", "expert"), None),
            P("expert", None, None),
            P("expert", None, None),
            P("expert", None, None),
        ),
        out_specs=(
            P(("dp", "expert"), None),
            P(("dp", "expert"), None),
            P(("dp", "expert"), None),
            P("expert", "dp", None),
            P("expert", "dp", None),
            P("expert", None, "dp"),
        ),
        check_vma=False,
    )
```
